512 devices in a mesh: ctx: 128 (over x_hi, y, z), head: 4 (over x_lo, core).
Axes of the slice: x: 4 (x_hi: 2, x_lo: 2; x = x_hi * 2 + x_lo), y: 8, z: 8, core: 2. Of those that a mesh axis runs over, the one named last changes fastest.
Arguments:
- queries: bfloat16 [16384, 2048], P('ctx', 'head'), may hold values from -6 to 6
- new_keys: bfloat16 [16384, 128], P('ctx'), may hold values from -6 to 6
- new_values: bfloat16 [16384, 128], P('ctx'), may hold values from -6 to 6
- cache_keys: bfloat16 [8192, 128], P('ctx'), may hold values from -9 to 9
- cache_values: bfloat16 [8192, 128], P('ctx'), may hold values from -6 to 6
- q_request: int32 [16384], replicated, may hold values from 0 to 3, never falling along the last dimension, each value on 1 to 8192 neighbouring positions
- block_request: int32 [512], replicated, may hold values from 0 to 3
Outputs:
- attention: bfloat16 [16384, 2048], P('ctx', 'head')
The draws below stay inside these ranges and needn't reach their ends.
Inputs may be any that keep to these rules, and one draw needn't show every extreme that they name: `q_request`: request numbers never fall along the rows; each of the 4 requests has one row or more, and one has exactly 8192.
All inputs are finite; a program needn't handle non-finite values.
Results may differ from the reference program's by a relative error of at most 0.006.
Values may be sent and summed in bfloat16 or wider, within the bound.
No kernel may reach another device: no remote copies, remote signals or barrier semaphores. Data moves between devices by JAX's collectives and lax.ppermute only.
A program may use at most 64 MiB of HBM per device.

```python
import math
import jax
import jax.numpy as jnp
import numpy as np
from jax import lax

QH = 16
KVH = 1
HD = 128
REQS = 4
BLK = 16
TOKENS = 16384
CACHE = 8192
NBLK = 512


def draw_queries(key, part):
    key = jax.random.fold_in(key, 1)
    drawn = jnp.clip(1.5 * jax.random.normal(key, (TOKENS, QH * HD), jnp.float32), -6.0, 6.0)
    return drawn.astype(jnp.bfloat16)


def draw_new_keys(key, part):
    key = jax.random.fold_in(key, 2)
    drawn = jnp.clip(1.5 * jax.random.normal(key, (TOKENS, KVH * HD), jnp.float32), -6.0, 6.0)
    return drawn.astype(jnp.bfloat16)


def touch_ends(values, rng, least, top_value):
    index_at = [jax.random.randint(jax.random.fold_in(rng, axis), (), 0, length) for axis, length in enumerate(values.shape)]
    main_axis = values.shape.index(max(values.shape))
    neighbour = index_at[:main_axis] + [(index_at[main_axis] + 1) % values.shape[main_axis]] + index_at[main_axis + 1:]
    return values.at[tuple(index_at)].set(least).at[tuple(neighbour)].set(top_value)


def block_scale(key, shape, split, low, high):
    loudness, own = 1.0, jax.random.fold_in(key, 6)
    for axis_at, parts in split:
        heights = jnp.exp(jax.random.uniform(jax.random.fold_in(own, axis_at), (parts,), jnp.float32, low / len(split), high / len(split)))
        loudness = loudness * jnp.repeat(heights, shape[axis_at] // parts).reshape([-1 if axis == axis_at else 1 for axis in range(len(shape))])
    return loudness


def cumulative_ranks(number_of, lean):
    portions = [(1 << 20) // math.isqrt(grade ** lean) + 1 for grade in range(1, number_of + 1)]
    spread = 1 + sum(portions) // (1 << 30)
    return np.cumsum(np.array([max(1, weight // spread) for weight in portions]))


def ranked_ids(stream_key, shape, number_of, skew):
    table = cumulative_ranks(number_of, skew)
    lot = jax.random.randint(jax.random.fold_in(stream_key, 1), shape, 0, int(table[number_of - 1]))
    grade = jnp.searchsorted(jnp.asarray(table, jnp.int32), lot, side="right")
    return jax.random.permutation(jax.random.fold_in(stream_key, 2), number_of)[grade].astype(jnp.int32)


def split_up(amount, total, limit, slope):
    weights = [(1 << 20) // math.isqrt(rank ** slope) + 1 for rank in range(2, amount + 1)]
    surplus, holding = total - limit - (amount - 1), [1] * (amount - 1)
    while surplus > 0:
        candidates = [i for i in range(amount - 1) if holding[i] < limit]
        pool, remaining = sum([weights[i] for i in candidates]), surplus
        for i in candidates:
            extra = min(limit - holding[i], max(1, remaining * weights[i] // pool), surplus)
            holding[i] = holding[i] + extra
            surplus = surplus - extra
    return np.array([limit] + holding)


def ragged(own_key, number_of, total, most, lean):
    if number_of == 2:
        one = jax.random.randint(own_key, (), max(1, total - most), min(most, total - 1) + 1)
        return jnp.stack([one, total - one])
    tallies = jnp.asarray(split_up(number_of, total, most, lean), jnp.int32)
    twos = (number_of - 1) // 2
    source_of, taker = tallies[1:1 + 2 * twos:2], tallies[2:2 + 2 * twos:2]
    slack = jnp.minimum(source_of - 1, most - taker)
    shifted = jax.random.randint(jax.random.fold_in(own_key, 1), (twos,), 0, 1 << 20) % (slack + 1)
    tallies = tallies.at[1:1 + 2 * twos:2].set(source_of - shifted).at[2:2 + 2 * twos:2].set(taker + shifted)
    return tallies[jax.random.permutation(jax.random.fold_in(own_key, 2), number_of)]


def gaussian(own_key, shape, deviation, most, split=(), kind=jnp.bfloat16):
    level = block_scale(own_key, shape, split, -0.22, 0.18) if split else 1.0
    values = jax.random.normal(own_key, shape, jnp.float32) * deviation * level
    return jnp.minimum(jnp.maximum(values, -most), most).astype(kind)


def setup_inputs(seed: int = 0) -> dict:
    splits = jax.random.split(jax.random.key(seed), 8)
    return {
        "queries": draw_queries(jax.random.fold_in(splits[7], 71), 0),
        "new_keys": draw_new_keys(jax.random.fold_in(splits[7], 71), 0),
        "new_values": gaussian(splits[2], (TOKENS, KVH * HD), 1.0, 6.0, ((0, 128),)),
        "cache_keys": gaussian(splits[3], (CACHE, KVH * HD), 1.5, 9.0, ((0, 128),)),
        "cache_values": gaussian(splits[4], (CACHE, KVH * HD), 1.0, 6.0, ((0, 128),)),
        "q_request": jnp.searchsorted(jnp.cumsum(ragged(splits[5], REQS, TOKENS, TOKENS // 2, 2)), jnp.arange(TOKENS), side="right").astype(jnp.int32),
        "block_request": touch_ends(ranked_ids(splits[6], (NBLK,), REQS, 2), jax.random.fold_in(splits[6], 3), 0, REQS - 1).astype(jnp.int32),
    }


masked_score = -1.0e30


def reference(queries, new_keys, new_values, cache_keys, cache_values, q_request, block_request):
    group_size = QH // KVH
    block_rows = min(128, TOKENS)
    score_scale = HD ** -0.5
    key_request = jnp.concatenate([jnp.repeat(block_request, BLK), q_request]).astype(jnp.int32)
    key_position = jnp.concatenate([jnp.full((CACHE,), -1, jnp.int32), jnp.arange(TOKENS, dtype=jnp.int32)])
    keys_all = jnp.concatenate([cache_keys, new_keys], axis=0).astype(jnp.float32).reshape(CACHE + TOKENS, KVH, HD)
    values_all = jnp.concatenate([cache_values, new_values], axis=0).astype(jnp.float32).reshape(CACHE + TOKENS, KVH, HD)

    def one_block(number):
        first_row = (number * block_rows).astype(jnp.int32)
        query_block = lax.dynamic_slice_in_dim(queries, first_row, block_rows, 0).astype(jnp.float32)
        query_block = query_block.reshape(block_rows, KVH, group_size, HD)
        requests = lax.dynamic_slice_in_dim(q_request, first_row, block_rows, 0)
        positions = first_row + jnp.arange(block_rows, dtype=jnp.int32)
        allowed = (requests[:, None] == key_request[None, :]) & (key_position[None, :] <= positions[:, None])
        scores = jnp.einsum("qhgd,khd->hgqk", query_block, keys_all) * score_scale
        scores = jnp.where(allowed, scores, masked_score)
        row_max = jnp.max(scores, axis=-1, keepdims=True)
        weights = jnp.where(allowed, jnp.exp(scores - row_max), 0.0)
        row_sum = jnp.sum(weights, axis=-1)
        rounded = lax.optimization_barrier(weights.astype(jnp.bfloat16)).astype(jnp.float32)
        output_sum = jnp.einsum("hgqk,khd->qhgd", rounded, values_all)
        result = output_sum / jnp.transpose(row_sum, (2, 0, 1))[..., None]
        return result.reshape(block_rows, QH * HD).astype(jnp.bfloat16)

    blocks = lax.map(one_block, jnp.arange(TOKENS // block_rows, dtype=jnp.int32))
    return blocks.reshape(TOKENS, QH * HD)
```

```python
import functools
import math

import jax
import jax.numpy as jnp
from jax import lax
from jax.experimental import pallas as pl
from jax.experimental.pallas import tpu as pltpu
from jax.sharding import Mesh, PartitionSpec as P

HD = 128
BLK = 16
ROWS = 128
CROWS = 64
HEADS = 4
SRC = 64
NEWK = 32
SLOT = NEWK + BLK
GROUP = 8
CHUNK = 512
NEW0 = SRC * BLK + CHUNK
KEYS = NEW0 + SRC * NEWK + CHUNK
LOW = -1.0e30
SCALE2 = math.log2(math.e) / math.sqrt(HD)
PIECE = HEADS * ROWS
STAT = 16

f32, bf16, i32 = jnp.float32, jnp.bfloat16, jnp.int32
VMEM = pl.BlockSpec(memory_space=pltpu.VMEM)
SMEM = pl.BlockSpec(memory_space=pltpu.SMEM)


def pick(index, values):
    out = values[-1]
    for at in range(len(values) - 2, -1, -1):
        out = jnp.where(index == at, values[at], out)
    return out


def prep_kernel(coord, blocks, requests, lo_ref, hi_ref, code_ref, pos, info):
    xh, y, zh, z0, xl = (coord[i] for i in range(5))
    part = xl * 2 + z0
    req = requests[...]
    starts = [jnp.int32(0)] + [
        jnp.sum(jnp.where(req < r, 1.0, 0.0).astype(f32)).astype(i32) for r in (1, 2, 3)
    ]

    def count(i, carry):
        r = blocks[(xh * SRC + i) * 4 + part]
        return tuple(c + jnp.where(r == k, 1, 0) for k, c in enumerate(carry))

    zero = jnp.int32(0)
    n = lax.fori_loop(0, SRC, count, (zero,) * 4)
    offs = [zero, n[0], n[0] + n[1], n[0] + n[1] + n[2], jnp.int32(SRC)]

    def place(i, carry):
        r = blocks[(xh * SRC + i) * 4 + part]
        pos[i] = pick(r, carry)
        return tuple(c + jnp.where(r == k, 1, 0) for k, c in enumerate(carry))

    lax.fori_loop(0, SRC, place, tuple(offs[:4]))

    lane = lax.broadcasted_iota(i32, (1, ROWS), 1)
    for tb in range(4):
        own = (tb // 2) * SRC + y * 8 + zh * 2 + tb % 2
        row = requests[pl.ds(own, 1), :]
        rowf = row.astype(f32)
        first = jnp.min(rowf).astype(i32)
        last = jnp.max(rowf).astype(i32)
        lo = 2 * pick(row, starts)
        hi = 2 * (own * ROWS + lane) + 1
        lo_ref[tb] = jnp.broadcast_to(lo.astype(f32), (ROWS, ROWS)).T
        hi_ref[tb] = jnp.broadcast_to(hi.astype(f32), (ROWS, ROWS)).T
        clo = pick(first, offs[:4]) * BLK
        chi = pick(last, offs[1:]) * BLK
        cs = (clo >> 7) << 7
        info[tb * 4 + 0] = cs
        info[tb * 4 + 1] = jnp.where(chi > clo, (chi - cs + CHUNK - 1) // CHUNK, 0)
        base = xh * SRC
        a = jnp.maximum(pick(first, starts) >> 7, base)
        b = jnp.minimum(own, base + SRC - 1)
        ns = (((a - base) * NEWK) >> 7) << 7
        end = (b - base + 1) * NEWK
        info[tb * 4 + 2] = NEW0 + ns
        info[tb * 4 + 3] = jnp.where(a <= b, (end - ns + CHUNK - 1) // CHUNK, 0)

    key = lax.broadcasted_iota(i32, (8, KEYS), 1)
    block = key >> 4
    cached = jnp.where(
        block >= offs[3],
        starts[3],
        jnp.where(block >= offs[2], starts[2], jnp.where(block >= offs[1], starts[1], 0)),
    )
    u = key - NEW0
    fresh = ROWS * (xh * SRC + (u >> 5)) + NEWK * part + (u & (NEWK - 1))
    code = jnp.where(key < SRC * BLK, 2 * cached, -1)
    code = jnp.where((u >= 0) & (u < SRC * NEWK), 2 * fresh + 1, code)
    code_ref[...] = code.astype(f32)


def attend_kernel(
    coord, pos, info, q_ref, own_ref, got_ref, lo_ref, hi_ref, code_ref, o_ref,
    kbuf, vbuf, qs, m_s, l_s, acc,
):
    for buf in (kbuf, vbuf):
        buf[pl.ds(SRC * BLK, CHUNK), :] = jnp.zeros((CHUNK, HD), bf16)
        buf[pl.ds(KEYS - CHUNK, CHUNK), :] = jnp.zeros((CHUNK, HD), bf16)

    def fill(buf, ref):
        buf[pl.ds(NEW0, SRC * NEWK), :] = ref[:, :NEWK, :].reshape(SRC * NEWK, HD)
        for i in range(SRC):
            to = pl.multiple_of(pos[i] * BLK, BLK)
            buf[pl.ds(to, BLK), :] = ref[i, NEWK:, :]

    @pl.when(coord[5] == 0)
    def _():
        fill(kbuf, own_ref)
        fill(vbuf, got_ref)

    @pl.when(coord[5] == 1)
    def _():
        fill(kbuf, got_ref)
        fill(vbuf, own_ref)

    lane = lax.broadcasted_iota(i32, (ROWS, ROWS), 1)

    def piece_step(piece, unused):
        tb = (piece // 4) * 2 + piece % 2
        for h in range(HEADS):
            qs[pl.ds(h * ROWS, ROWS), :] = q_ref[piece, :, h * HD : (h + 1) * HD]
        m_s[...] = jnp.full(m_s.shape, LOW, f32)
        l_s[...] = jnp.zeros(l_s.shape, f32)
        acc[...] = jnp.zeros(acc.shape, f32)
        cs, nc, ns, nn = (info[tb * 4 + i] for i in range(4))

        def chunk_step(j, unused):
            at = jnp.where(j < nc, cs + j * CHUNK, ns + (j - nc) * CHUNK)
            at = pl.multiple_of(at, 128)
            k = kbuf[pl.ds(at, CHUNK), :]
            v = vbuf[pl.ds(at, CHUNK), :]
            code = code_ref[0:1, pl.ds(at, CHUNK)]
            lo, hi = lo_ref[tb], hi_ref[tb]
            bias = jnp.concatenate(
                [
                    jnp.where((c >= lo) & (c <= hi), 0.0, LOW)
                    for c in (code[:, g * 128 : (g + 1) * 128] for g in range(CHUNK // 128))
                ],
                axis=1,
            )
            s = lax.dot_general(qs[...], k, (((1,), (1,)), ((), ())), preferred_element_type=f32)
            probs, alphas = [], []
            for h in range(HEADS):
                rows = pl.ds(h * ROWS, ROWS)
                sh = s[h * ROWS : (h + 1) * ROWS] + bias
                old = m_s[rows, :]
                new = jnp.maximum(old, jnp.max(sh, axis=1, keepdims=True))
                p = jnp.exp2((sh - new) * SCALE2)
                alpha = jnp.exp2((old - new) * SCALE2)
                m_s[rows, :] = new
                l_s[rows, :] = l_s[rows, :] * alpha + jnp.sum(p, axis=1, keepdims=True)
                probs.append(p.astype(bf16))
                alphas.append(alpha)
            pv = lax.dot_general(
                jnp.concatenate(probs, axis=0), v, (((1,), (0,)), ((), ())), preferred_element_type=f32
            )
            for h in range(HEADS):
                rows = pl.ds(h * ROWS, ROWS)
                acc[rows, :] = acc[rows, :] * alphas[h] + pv[h * ROWS : (h + 1) * ROWS]
            return unused

        lax.fori_loop(0, nc + nn, chunk_step, 0)
        stat = jnp.zeros((ROWS, ROWS), f32)
        for h in range(HEADS):
            rows = pl.ds(h * ROWS, ROWS)
            total = l_s[rows, :]
            total = jnp.where(total > 0.0, total, 1.0)
            o_ref[piece, rows, :] = (acc[rows, :] / total).astype(bf16)
            lse = m_s[rows, :] * SCALE2 + jnp.log2(total)
            stat = jnp.where(lane == h, lse, stat)
        stat = stat.T[:HEADS]
        top = stat.astype(bf16)
        rest = stat - top.astype(f32)
        mid = rest.astype(bf16)
        low = (rest - mid.astype(f32)).astype(bf16)
        o_ref[piece, pl.ds(PIECE, STAT), :] = jnp.concatenate(
            [top.astype(f32), mid.astype(f32), low.astype(f32), jnp.zeros((HEADS, ROWS), f32)], axis=0
        ).astype(bf16)
        return unused

    lax.fori_loop(0, GROUP, piece_step, 0)


def combine_kernel(r_ref, out_ref):
    parts = []
    for i in range(GROUP):
        stat = r_ref[i, pl.ds(PIECE, STAT), :].astype(f32)
        parts.append(stat[0:4] + stat[4:8] + stat[8:12])
    best = functools.reduce(jnp.maximum, parts)
    weights = [jnp.exp2(part - best) for part in parts]
    total = functools.reduce(jnp.add, weights)
    inverse = 1.0 / total
    table = jnp.concatenate([w * inverse for w in weights] + [jnp.zeros((96, ROWS), f32)], axis=0).T
    for h in range(HEADS):
        out = jnp.zeros((ROWS, HD), f32)
        for i in range(GROUP):
            at = i * HEADS + h
            out = out + table[:, at : at + 1] * r_ref[i, pl.ds(h * ROWS, ROWS), :].astype(f32)
        out_ref[:, h * HD : (h + 1) * HD] = out.astype(bf16)


def body(queries, new_keys, new_values, cache_keys, cache_values, q_request, block_request):
    axes = ("xh", "y", "zh", "z0", "xl", "core")
    where = [lax.axis_index(a) for a in axes]
    core, xl = where[5], where[4]
    coord = jnp.stack(where + [jnp.int32(0)] * 2).astype(i32)

    new = jnp.where(core == 0, new_keys, new_values).reshape(2, 2, NEWK, HD)
    old = jnp.where(core == 0, cache_keys, cache_values).reshape(2, 2, BLK, HD)
    both = jnp.concatenate([new, old], axis=2)
    both = jnp.where(xl == 0, both[0], both[1])
    slots = jnp.broadcast_to(both[None], (SRC // 2, 2, SLOT, HD)).reshape(SRC, SLOT, HD)
    held = lax.all_to_all(slots, ("y", "zh", "z0"), 0, 0)
    q_all = lax.all_gather(queries, ("xh", "xl", "z0"), axis=0, tiled=False)

    lo, hi, code, pos, info = pl.pallas_call(
        prep_kernel,
        out_shape=(
            jax.ShapeDtypeStruct((4, ROWS, ROWS), f32),
            jax.ShapeDtypeStruct((4, ROWS, ROWS), f32),
            jax.ShapeDtypeStruct((8, KEYS), f32),
            jax.ShapeDtypeStruct((SRC,), i32),
            jax.ShapeDtypeStruct((16,), i32),
        ),
        in_specs=[SMEM, SMEM, VMEM],
        out_specs=(VMEM, VMEM, VMEM, SMEM, SMEM),
        cost_estimate=pl.CostEstimate(flops=1000000, bytes_accessed=800000, transcendentals=0),
        name="prep",
    )(coord, block_request, q_request.reshape(ROWS, ROWS))

    got = lax.ppermute(held, "core", [(0, 1), (1, 0)])
    partial = pl.pallas_call(
        attend_kernel,
        out_shape=jax.ShapeDtypeStruct((GROUP, PIECE + STAT, HD), bf16),
        in_specs=[SMEM, SMEM, SMEM] + [VMEM] * 6,
        out_specs=VMEM,
        scratch_shapes=[
            pltpu.VMEM((KEYS, HD), bf16),
            pltpu.VMEM((KEYS, HD), bf16),
            pltpu.VMEM((PIECE, HD), bf16),
            pltpu.VMEM((PIECE, 1), f32),
            pltpu.VMEM((PIECE, 1), f32),
            pltpu.VMEM((PIECE, HD), f32),
        ],
        compiler_params=pltpu.CompilerParams(vmem_limit_bytes=32 * 1024 * 1024),
        cost_estimate=pl.CostEstimate(flops=4 * 8000000 * HD, bytes_accessed=4000000, transcendentals=8000000),
        name="attend",
    )(coord, pos, info, q_all, held, got, lo, hi, code)

    shared = lax.all_to_all(partial, ("xh", "xl", "z0"), 0, 0)
    return pl.pallas_call(
        combine_kernel,
        out_shape=jax.ShapeDtypeStruct((ROWS, HEADS * HD), bf16),
        in_specs=[VMEM],
        out_specs=VMEM,
        compiler_params=pltpu.CompilerParams(vmem_limit_bytes=16 * 1024 * 1024),
        name="combine",
    )(shared)


def solution(mesh):
    fine = Mesh(mesh.devices.reshape(2, 8, 4, 2, 2, 2), ("xh", "y", "zh", "z0", "xl", "core"))
    ctx, head = ("xh", "y", "zh", "z0"), ("xl", "core")
    return jax.shard_map(
        body,
        mesh=fine,
        in_specs=(P(ctx, head), P(ctx, None), P(ctx, None), P(ctx, None), P(ctx, None), P(), P()),
        out_specs=P(ctx, head),
        check_vma=False,
    )
```

```python
import functools
import math

import jax
import jax.numpy as jnp
from jax import lax
from jax.experimental import pallas as pl
from jax.experimental.pallas import tpu as pltpu
from jax.sharding import Mesh, PartitionSpec as P

HD = 128
BLK = 16
ROWS = 128
HEADS = 4
SRC = 64
NEWK = 32
OLDK = 16
PER = OLDK // BLK
SLOT = NEWK + OLDK
GROUP = 8
TBS = 4
SUB1, SUB2 = 256, 256
UNITS = 4
CHUNK = 256
NEW0 = SRC * OLDK + CHUNK
KEYS = NEW0 + SRC * NEWK + CHUNK
STEPS = (SRC * OLDK + SRC * NEWK) // CHUNK
LOW = -1.0e30
SCALE2 = math.log2(math.e) / math.sqrt(HD)
PIECE = HEADS * ROWS
STAT = 16
LO0, HI0, CODE0 = 0, TBS * ROWS, 2 * TBS * ROWS
META = CODE0 + (KEYS // 128 + 7) // 8 * 8
BLOCKS = SRC * PER
TB0, CO0, INFO = BLOCKS, BLOCKS + 4 * TBS, BLOCKS + 4 * TBS + 8

f32, bf16, i32 = jnp.float32, jnp.bfloat16, jnp.int32
VMEM = pl.BlockSpec(memory_space=pltpu.VMEM)
SMEM = pl.BlockSpec(memory_space=pltpu.SMEM)


def pick(index, values):
    out = values[-1]
    for at in range(len(values) - 2, -1, -1):
        out = jnp.where(index == at, values[at], out)
    return out


def prep_kernel(coord, blocks, requests, meta, info):
    xh, y, zh, z0, xl = (coord[i] for i in range(5))
    part = xl * 2 + z0
    for i in range(8):
        info[CO0 + i] = coord[i]
    req = requests[...]
    starts = [jnp.int32(0)] + [
        jnp.sum(jnp.where(req < r, 1.0, 0.0).astype(f32)).astype(i32) for r in (1, 2, 3)
    ]

    def count(i, carry):
        r = blocks[(xh * SRC + i // PER) * 4 + part * PER + i % PER]
        return tuple(c + jnp.where(r == k, 1, 0) for k, c in enumerate(carry))

    zero = jnp.int32(0)
    n = lax.fori_loop(0, BLOCKS, count, (zero,) * 4)
    offs = [zero, n[0], n[0] + n[1], n[0] + n[1] + n[2], jnp.int32(BLOCKS)]

    def place(i, carry):
        r = blocks[(xh * SRC + i // PER) * 4 + part * PER + i % PER]
        info[i] = pick(r, carry)
        return tuple(c + jnp.where(r == k, 1, 0) for k, c in enumerate(carry))

    lax.fori_loop(0, BLOCKS, place, tuple(offs[:4]))

    lane = lax.broadcasted_iota(i32, (1, ROWS), 1)
    for tb in range(TBS):
        own = (tb // 2) * SRC + y * 8 + zh * 2 + tb % 2
        row = requests[pl.ds(own, 1), :]
        rowf = row.astype(f32)
        first = jnp.min(rowf).astype(i32)
        last = jnp.max(rowf).astype(i32)
        lo = 2 * pick(row, starts)
        hi = 2 * (own * ROWS + lane) + 1
        meta[pl.ds(LO0 + tb * ROWS, ROWS), :] = jnp.broadcast_to(lo.astype(f32), (ROWS, ROWS)).T
        meta[pl.ds(HI0 + tb * ROWS, ROWS), :] = jnp.broadcast_to(hi.astype(f32), (ROWS, ROWS)).T
        clo = pick(first, offs[:4]) * BLK
        chi = pick(last, offs[1:]) * BLK
        cs = (clo >> 7) << 7
        info[TB0 + tb * 4 + 0] = cs
        info[TB0 + tb * 4 + 1] = jnp.where(chi > clo, (chi - cs + CHUNK - 1) // CHUNK, 0)
        base = xh * SRC
        a = jnp.maximum(pick(first, starts) >> 7, base)
        b = jnp.minimum(own, base + SRC - 1)
        ns = (((a - base) * NEWK) >> 7) << 7
        end = (b - base + 1) * NEWK
        info[TB0 + tb * 4 + 2] = NEW0 + ns
        info[TB0 + tb * 4 + 3] = jnp.where(a <= b, (end - ns + CHUNK - 1) // CHUNK, 0)

    shape = (META - CODE0, 128)
    key = lax.broadcasted_iota(i32, shape, 0) * 128 + lax.broadcasted_iota(i32, shape, 1)
    block = key >> 4
    cached = jnp.where(
        block >= offs[3],
        starts[3],
        jnp.where(block >= offs[2], starts[2], jnp.where(block >= offs[1], starts[1], 0)),
    )
    u = key - NEW0
    fresh = ROWS * (xh * SRC + (u >> 5)) + NEWK * part + (u & (NEWK - 1))
    code = jnp.where(key < SRC * OLDK, 2 * cached, -1)
    code = jnp.where((u >= 0) & (u < SRC * NEWK), 2 * fresh + 1, code)
    meta[pl.ds(CODE0, META - CODE0), :] = code.astype(f32)


def attend_kernel(info, *refs):
    q_refs, (own_ref, got_ref, meta, o_ref, kbuf, vbuf, qs, ss, mx, sm, acc) = refs[:4], refs[4:]
    for buf in (kbuf, vbuf):
        buf[pl.ds(SRC * OLDK, CHUNK), :] = jnp.zeros((CHUNK, HD), bf16)
        buf[pl.ds(KEYS - CHUNK, CHUNK), :] = jnp.zeros((CHUNK, HD), bf16)

    def fill(buf, ref):
        buf[pl.ds(NEW0, SRC * NEWK), :] = ref[:, :NEWK, :].reshape(SRC * NEWK, HD)
        for i in range(BLOCKS):
            to = pl.multiple_of(info[i] * BLK, BLK)
            buf[pl.ds(to, BLK), :] = ref[i // PER, pl.ds(NEWK + (i % PER) * BLK, BLK), :]

    @pl.when(info[CO0 + 5] == 0)
    def _():
        fill(kbuf, own_ref)
        fill(vbuf, got_ref)

    @pl.when(info[CO0 + 5] == 1)
    def _():
        fill(kbuf, got_ref)
        fill(vbuf, own_ref)

    xh, z0, xl = info[CO0 + 0], info[CO0 + 3], info[CO0 + 4]
    for d in range(4):
        for e in range(2):
            tb = (xh ^ (d >> 1)) * 2 + (z0 ^ e)
            for h in range(HEADS):
                at = pl.multiple_of((xl ^ (d & 1)) * PIECE + h * ROWS, ROWS)
                qs[tb, pl.ds(at, ROWS), :] = q_refs[d][pl.ds(e * ROWS, ROWS), h * HD : (h + 1) * HD]

    lane = lax.broadcasted_iota(i32, (ROWS, ROWS), 1)
    heads = range(2 * HEADS)

    def block_step(tb, unused):
        mx[...] = jnp.full(mx.shape, LOW, f32)
        sm[...] = jnp.zeros(sm.shape, f32)
        acc[...] = jnp.zeros(acc.shape, f32)
        cs, nc, ns, nn = (info[TB0 + tb * 4 + i] for i in range(4))

        def place(j):
            return pl.multiple_of(jnp.where(j < nc, cs + j * CHUNK, ns + (j - nc) * CHUNK), 128)

        def score_step(j, units):
            lo = meta[pl.ds(pl.multiple_of(LO0 + tb * ROWS, ROWS), ROWS), :]
            hi = meta[pl.ds(pl.multiple_of(HI0 + tb * ROWS, ROWS), ROWS), :]
            keys, bias = [], []
            for i in range(units):
                at = place(j + i)
                keys.append(kbuf[pl.ds(at, CHUNK), :])
                for g in range(CHUNK // 128):
                    code = meta[pl.ds(CODE0 + (at >> 7) + g, 1), :]
                    bias.append(jnp.where((code >= lo) & (code <= hi), 0.0, LOW))
            keys = jnp.concatenate(keys, axis=0)
            for h in heads:
                low = h * ROWS % SUB1
                if low == 0:
                    s = lax.dot_general(
                        qs[tb, pl.ds(h * ROWS, SUB1), :], keys, (((1,), (1,)), ((), ())), preferred_element_type=f32
                    )
                rows = pl.ds(h * ROWS, ROWS)
                best = mx[rows, :]
                for g in range(units * CHUNK // 128):
                    part = s[low : low + ROWS, g * 128 : (g + 1) * 128] * SCALE2 + bias[g]
                    ss[j + g // 2, rows, (g % 2) * 128 : (g % 2 + 1) * 128] = part
                    best = jnp.maximum(best, part)
                mx[rows, :] = best

        def sweep(step):
            n = nc + nn

            def most(i, unused):
                step(i * UNITS, UNITS)
                return unused

            lax.fori_loop(0, n // UNITS, most, 0)
            units = UNITS // 2
            while units:
                left = n % (2 * units)

                @pl.when(left >= units)
                def _(units=units, left=left):
                    step(n - left, units)

                units //= 2

        sweep(score_step)
        for h in heads:
            rows = pl.ds(h * ROWS, ROWS)
            mx[rows, :] = jnp.broadcast_to(jnp.max(mx[rows, :], axis=1, keepdims=True), (ROWS, 128))

        def value_step(j, units):
            v = jnp.concatenate([vbuf[pl.ds(place(j + i), CHUNK), :] for i in range(units)], axis=0)
            probs = []
            for h in heads:
                rows = pl.ds(h * ROWS, ROWS)
                best, total = mx[rows, :], sm[rows, :]
                parts = []
                for g in range(units * CHUNK // 128):
                    p = jnp.exp2(ss[j + g // 2, rows, (g % 2) * 128 : (g % 2 + 1) * 128] - best)
                    total = total + p
                    parts.append(p.astype(bf16))
                sm[rows, :] = total
                probs.append(jnp.concatenate(parts, axis=1))
                if len(probs) * ROWS == SUB2:
                    acc[pl.ds((h + 1) * ROWS - SUB2, SUB2), :] += lax.dot_general(
                        jnp.concatenate(probs, axis=0), v, (((1,), (0,)), ((), ())), preferred_element_type=f32
                    )
                    probs = []

        sweep(value_step)
        stat = jnp.zeros((ROWS, ROWS), f32)
        for h in heads:
            rows = pl.ds(h * ROWS, ROWS)
            piece = tb * 2 + h // HEADS
            total = jnp.sum(sm[rows, :], axis=1, keepdims=True)
            total = jnp.where(total > 0.0, total, 1.0)
            o_ref[piece, pl.ds((h % HEADS) * ROWS, ROWS), :] = (acc[rows, :] * (1.0 / total)).astype(bf16)
            lse = mx[rows, 0:1] + jnp.log2(total)
            stat = jnp.where(lane == h, lse, stat)
        stat = stat.T
        for half in range(2):
            piece = tb * 2 + half
            part = stat[half * HEADS : (half + 1) * HEADS]
            top = part.astype(bf16)
            rest = part - top.astype(f32)
            mid = rest.astype(bf16)
            low = (rest - mid.astype(f32)).astype(bf16)
            o_ref[piece, pl.ds(PIECE, STAT), :] = jnp.concatenate(
                [top.astype(f32), mid.astype(f32), low.astype(f32), jnp.zeros((HEADS, ROWS), f32)], axis=0
            ).astype(bf16)
        return unused

    lax.fori_loop(0, TBS, block_step, 0)


def attend(info, queries, held, got, meta):
    return pl.pallas_call(
        attend_kernel,
        out_shape=jax.ShapeDtypeStruct((GROUP, PIECE + STAT, HD), bf16),
        in_specs=[SMEM] + [VMEM] * 7,
        out_specs=VMEM,
        scratch_shapes=[
            pltpu.VMEM((KEYS, HD), bf16),
            pltpu.VMEM((KEYS, HD), bf16),
            pltpu.VMEM((TBS, 2 * PIECE, HD), bf16),
            pltpu.VMEM((STEPS, 2 * PIECE, CHUNK), f32),
            pltpu.VMEM((2 * PIECE, 128), f32),
            pltpu.VMEM((2 * PIECE, 128), f32),
            pltpu.VMEM((2 * PIECE, HD), f32),
        ],
        compiler_params=pltpu.CompilerParams(vmem_limit_bytes=44 * 1024 * 1024),
        cost_estimate=pl.CostEstimate(flops=4 * 8000000 * HD, bytes_accessed=4000000, transcendentals=8000000),
        name="attend",
    )(info, *queries, held, got, meta)


def combine_kernel(r_ref, out_ref):
    parts = []
    for i in range(GROUP):
        stat = r_ref[i, pl.ds(PIECE, STAT), :].astype(f32)
        parts.append(stat[0:4] + stat[4:8] + stat[8:12])
    best = functools.reduce(jnp.maximum, parts)
    weights = [jnp.exp2(part - best) for part in parts]
    total = functools.reduce(jnp.add, weights)
    inverse = 1.0 / total
    table = jnp.concatenate([w * inverse for w in weights] + [jnp.zeros((ROWS - GROUP * HEADS, ROWS), f32)], axis=0).T
    for h in range(HEADS):
        out = jnp.zeros((ROWS, HD), f32)
        for i in range(GROUP):
            at = i * HEADS + h
            out = out + table[:, at : at + 1] * r_ref[i, pl.ds(h * ROWS, ROWS), :].astype(f32)
        out_ref[:, h * HD : (h + 1) * HD] = out.astype(bf16)


def body(queries, new_keys, new_values, cache_keys, cache_values, q_request, block_request):
    axes = ("xh", "y", "zh", "z0", "xl", "core")
    where = [lax.axis_index(a) for a in axes]
    core, xl = where[5], where[4]
    coord = jnp.stack(where + [jnp.int32(0)] * 2).astype(i32)

    across = lax.ppermute(queries, "z0", [(0, 1), (1, 0)])
    new = jnp.where(core == 0, new_keys, new_values).reshape(2, 2, NEWK, HD)
    old = jnp.where(core == 0, cache_keys, cache_values).reshape(2, 2, OLDK, HD)
    both = jnp.concatenate([new, old], axis=2)
    both = jnp.where(xl == 0, both[0], both[1])
    slots = jnp.broadcast_to(both[None], (SRC // 2, 2, SLOT, HD)).reshape(SRC, SLOT, HD)
    slots, across = lax.optimization_barrier((slots, across))
    pair = jnp.concatenate([queries, across], axis=0)
    held = lax.all_to_all(slots, ("y", "zh", "z0"), 0, 0)
    shared = [pair] + [lax.ppermute(pair, ("xh", "xl"), [(i, i ^ d) for i in range(4)]) for d in range(1, 4)]
    meta, info = pl.pallas_call(
        prep_kernel,
        out_shape=(jax.ShapeDtypeStruct((META, 128), f32), jax.ShapeDtypeStruct((INFO,), i32)),
        in_specs=[SMEM, SMEM, VMEM],
        out_specs=(VMEM, SMEM),
        cost_estimate=pl.CostEstimate(flops=1000000, bytes_accessed=800000, transcendentals=0),
        name="prep",
    )(coord, block_request, q_request.reshape(ROWS, ROWS))
    held, meta, info, *shared = lax.optimization_barrier((held, meta, info, *shared))
    got = lax.ppermute(held, "core", [(0, 1), (1, 0)])
    partial = attend(info, shared, held, got, meta)
    parts = lax.all_to_all(partial, ("xh", "z0", "xl"), 0, 0)
    return pl.pallas_call(
        combine_kernel,
        out_shape=jax.ShapeDtypeStruct((ROWS, HEADS * HD), bf16),
        in_specs=[VMEM],
        out_specs=VMEM,
        compiler_params=pltpu.CompilerParams(vmem_limit_bytes=16 * 1024 * 1024),
        name="combine",
    )(parts)


def solution(mesh):
    fine = Mesh(mesh.devices.reshape(2, 8, 4, 2, 2, 2), ("xh", "y", "zh", "z0", "xl", "core"))
    ctx, head = ("xh", "y", "zh", "z0"), ("xl", "core")
    return jax.shard_map(
        body,
        mesh=fine,
        in_specs=(P(ctx, head), P(ctx, None), P(ctx, None), P(ctx, None), P(ctx, None), P(), P()),
        out_specs=P(ctx, head),
        check_vma=False,
    )
```

```python
import functools
import math

import jax
import jax.numpy as jnp
from jax import lax
from jax.experimental import pallas as pl
from jax.experimental.pallas import tpu as pltpu
from jax.sharding import Mesh, PartitionSpec as P

HD = 128
BLK = 16
ROWS = 128
HEADS = 4
SRC = 64
NEWK = 32
OLDK = 16
PER = OLDK // BLK
SLOT = NEWK + OLDK
GROUP = 8
TBS = 4
PAIRS = TBS // 2
SUB1, SUB2 = 256, 256
UNITS = 4
CHUNK = 256
NEW0 = SRC * OLDK + CHUNK
KEYS = NEW0 + SRC * NEWK + CHUNK
STEPS = (SRC * OLDK + SRC * NEWK) // CHUNK
LOW = -1.0e30
SCALE2 = math.log2(math.e) / math.sqrt(HD)
PIECE = HEADS * ROWS
PROWS = 4 * PIECE
STAT = 16
LO0, HI0, CODE0 = 0, TBS * ROWS, 2 * TBS * ROWS
META = CODE0 + (KEYS // 128 + 7) // 8 * 8
BLOCKS = SRC * PER
TB0, CO0, INFO = BLOCKS, BLOCKS + 4 * PAIRS, BLOCKS + 4 * PAIRS + 8

f32, bf16, i32 = jnp.float32, jnp.bfloat16, jnp.int32
VMEM = pl.BlockSpec(memory_space=pltpu.VMEM)
SMEM = pl.BlockSpec(memory_space=pltpu.SMEM)
ANY = pl.BlockSpec(memory_space=pl.ANY)


def pick(index, values):
    out = values[-1]
    for at in range(len(values) - 2, -1, -1):
        out = jnp.where(index == at, values[at], out)
    return out


def prep_kernel(coord, blocks, requests, meta, info):
    xh, y, zh, z0, xl = (coord[i] for i in range(5))
    part = xl * 2 + z0
    for i in range(8):
        info[CO0 + i] = coord[i]
    req = requests[...]
    starts = [jnp.int32(0)] + [
        jnp.sum(jnp.where(req < r, 1.0, 0.0).astype(f32)).astype(i32) for r in (1, 2, 3)
    ]

    def count(i, carry):
        r = blocks[(xh * SRC + i // PER) * 4 + part * PER + i % PER]
        return tuple(c + jnp.where(r == k, 1, 0) for k, c in enumerate(carry))

    zero = jnp.int32(0)
    n = lax.fori_loop(0, BLOCKS, count, (zero,) * 4)
    offs = [zero, n[0], n[0] + n[1], n[0] + n[1] + n[2], jnp.int32(BLOCKS)]

    def place(i, carry):
        r = blocks[(xh * SRC + i // PER) * 4 + part * PER + i % PER]
        info[i] = pick(r, carry)
        return tuple(c + jnp.where(r == k, 1, 0) for k, c in enumerate(carry))

    lax.fori_loop(0, BLOCKS, place, tuple(offs[:4]))

    lane = lax.broadcasted_iota(i32, (1, ROWS), 1)
    for pair in range(PAIRS):
        firsts, lasts = [], []
        for e in range(2):
            tb, own = pair * 2 + e, pair * SRC + y * 8 + zh * 2 + e
            row = requests[pl.ds(own, 1), :]
            rowf = row.astype(f32)
            firsts.append(jnp.min(rowf).astype(i32))
            lasts.append(jnp.max(rowf).astype(i32))
            lo = 2 * pick(row, starts)
            hi = 2 * (own * ROWS + lane) + 1
            meta[pl.ds(LO0 + tb * ROWS, ROWS), :] = jnp.broadcast_to(lo.astype(f32), (ROWS, ROWS)).T
            meta[pl.ds(HI0 + tb * ROWS, ROWS), :] = jnp.broadcast_to(hi.astype(f32), (ROWS, ROWS)).T
        first, last = firsts[0], lasts[1]
        clo = pick(first, offs[:4]) * BLK
        chi = pick(last, offs[1:]) * BLK
        cs = (clo >> 7) << 7
        info[TB0 + pair * 4 + 0] = cs
        info[TB0 + pair * 4 + 1] = jnp.where(chi > clo, (chi - cs + CHUNK - 1) // CHUNK, 0)
        base = xh * SRC
        a = jnp.maximum(pick(first, starts) >> 7, base)
        b = jnp.minimum(own, base + SRC - 1)
        ns = (((a - base) * NEWK) >> 7) << 7
        end = (b - base + 1) * NEWK
        info[TB0 + pair * 4 + 2] = NEW0 + ns
        info[TB0 + pair * 4 + 3] = jnp.where(a <= b, (end - ns + CHUNK - 1) // CHUNK, 0)

    shape = (META - CODE0, 128)
    key = lax.broadcasted_iota(i32, shape, 0) * 128 + lax.broadcasted_iota(i32, shape, 1)
    block = key >> 4
    cached = jnp.where(
        block >= offs[3],
        starts[3],
        jnp.where(block >= offs[2], starts[2], jnp.where(block >= offs[1], starts[1], 0)),
    )
    u = key - NEW0
    fresh = ROWS * (xh * SRC + (u >> 5)) + NEWK * part + (u & (NEWK - 1))
    code = jnp.where(key < SRC * OLDK, 2 * cached, -1)
    code = jnp.where((u >= 0) & (u < SRC * NEWK), 2 * fresh + 1, code)
    meta[pl.ds(CODE0, META - CODE0), :] = code.astype(f32)


def attend_kernel(info_in, *refs):
    q_refs, refs = refs[:4], refs[4:]
    own_ref, got_ref, meta_in, o_ref, info, meta, sem, kbuf, vbuf, qs, ss, mx, acc = refs
    copy_info = pltpu.make_async_copy(info_in, info, sem.at[0])
    copy_meta = pltpu.make_async_copy(meta_in, meta, sem.at[1])
    copy_info.start()
    copy_meta.start()
    for at in (SRC * OLDK, KEYS - CHUNK):
        kbuf[pl.ds(at, CHUNK), :] = jnp.zeros((CHUNK, HD), bf16)
        vbuf[pl.ds(at, CHUNK), :HD] = jnp.zeros((CHUNK, HD), bf16)
    vbuf[:, HD:] = jnp.ones((KEYS, HD), bf16)
    copy_info.wait()

    def fill(buf, ref):
        buf[pl.ds(NEW0, SRC * NEWK), :HD] = ref[:, :NEWK, :].reshape(SRC * NEWK, HD)
        for i in range(BLOCKS):
            to = pl.multiple_of(info[i] * BLK, BLK)
            buf[pl.ds(to, BLK), :HD] = ref[i // PER, pl.ds(NEWK + (i % PER) * BLK, BLK), :]

    @pl.when(info[CO0 + 5] == 0)
    def _():
        fill(kbuf, own_ref)
        fill(vbuf, got_ref)

    @pl.when(info[CO0 + 5] == 1)
    def _():
        fill(kbuf, got_ref)
        fill(vbuf, own_ref)

    xh, z0, xl = info[CO0 + 0], info[CO0 + 3], info[CO0 + 4]
    for d in range(4):
        for e in range(2):
            for h in range(HEADS):
                at = pl.multiple_of(((z0 ^ e) * 2 + (xl ^ (d & 1))) * PIECE + h * ROWS, ROWS)
                qs[xh ^ (d >> 1), pl.ds(at, ROWS), :] = q_refs[d][pl.ds(e * ROWS, ROWS), h * HD : (h + 1) * HD]

    lane = lax.broadcasted_iota(i32, (ROWS, ROWS), 1)
    heads = range(4 * HEADS)
    copy_meta.wait()

    def pair_step(pair, unused):
        mx[...] = jnp.full(mx.shape, LOW, f32)
        acc[...] = jnp.zeros(acc.shape, f32)
        cs, nc, ns, nn = (info[TB0 + pair * 4 + i] for i in range(4))

        def place(j):
            return pl.multiple_of(jnp.where(j < nc, cs + j * CHUNK, ns + (j - nc) * CHUNK), 128)

        def score_step(j, units):
            keys, bias = [], ([], [])
            for i in range(units):
                at = place(j + i)
                keys.append(kbuf[pl.ds(at, CHUNK), :])
                for g in range(CHUNK // 128):
                    code = meta[pl.ds(CODE0 + (at >> 7) + g, 1), :]
                    for e in range(2):
                        line = (pair * 2 + e) * ROWS
                        lo = meta[pl.ds(pl.multiple_of(LO0 + line, ROWS), ROWS), :]
                        hi = meta[pl.ds(pl.multiple_of(HI0 + line, ROWS), ROWS), :]
                        bias[e].append(jnp.where((code >= lo) & (code <= hi), 0.0, LOW))
            keys = jnp.concatenate(keys, axis=0)
            for h in heads:
                low = h * ROWS % SUB1
                if low == 0:
                    s = lax.dot_general(
                        qs[pair, pl.ds(h * ROWS, SUB1), :], keys, (((1,), (1,)), ((), ())), preferred_element_type=f32
                    )
                rows = pl.ds(h * ROWS, ROWS)
                best = mx[rows, :]
                for g in range(units * CHUNK // 128):
                    part = s[low : low + ROWS, g * 128 : (g + 1) * 128] * SCALE2 + bias[h // 8][g]
                    ss[j + g // 2, rows, (g % 2) * 128 : (g % 2 + 1) * 128] = part
                    best = jnp.maximum(best, part)
                mx[rows, :] = best

        def sweep(step):
            n = nc + nn

            def most(i, unused):
                step(i * UNITS, UNITS)
                return unused

            lax.fori_loop(0, n // UNITS, most, 0)
            units = UNITS // 2
            while units:
                left = n % (2 * units)

                @pl.when(left >= units)
                def _(units=units, left=left):
                    step(n - left, units)

                units //= 2

        sweep(score_step)
        for h in heads:
            rows = pl.ds(h * ROWS, ROWS)
            mx[rows, :] = jnp.broadcast_to(jnp.max(mx[rows, :], axis=1, keepdims=True), (ROWS, 128))

        def value_step(j, units):
            v = jnp.concatenate([vbuf[pl.ds(place(j + i), CHUNK), :] for i in range(units)], axis=0)
            probs = []
            for h in heads:
                rows = pl.ds(h * ROWS, ROWS)
                best = mx[rows, :]
                parts = []
                for g in range(units * CHUNK // 128):
                    p = jnp.exp2(ss[j + g // 2, rows, (g % 2) * 128 : (g % 2 + 1) * 128] - best)
                    parts.append(p.astype(bf16))
                probs.append(jnp.concatenate(parts, axis=1))
                if len(probs) * ROWS == SUB2:
                    acc[pl.ds((h + 1) * ROWS - SUB2, SUB2), :] += lax.dot_general(
                        jnp.concatenate(probs, axis=0), v, (((1,), (0,)), ((), ())), preferred_element_type=f32
                    )
                    probs = []

        sweep(value_step)
        stat = jnp.zeros((ROWS, ROWS), f32)
        for h in heads:
            rows = pl.ds(h * ROWS, ROWS)
            total = acc[rows, HD:]
            total = jnp.where(total > 0.0, total, 1.0)
            o_ref[pair * 4 + h // HEADS, pl.ds((h % HEADS) * ROWS, ROWS), :] = (acc[rows, :HD] / total).astype(bf16)
            stat = jnp.where(lane == h, mx[rows, :] + jnp.log2(total), stat)
        stat = stat.T
        for i in range(4):
            part = stat[i * HEADS : (i + 1) * HEADS]
            top = part.astype(bf16)
            rest = part - top.astype(f32)
            mid = rest.astype(bf16)
            low = (rest - mid.astype(f32)).astype(bf16)
            o_ref[pair * 4 + i, pl.ds(PIECE, STAT), :] = jnp.concatenate(
                [top.astype(f32), mid.astype(f32), low.astype(f32), jnp.zeros((HEADS, ROWS), f32)], axis=0
            ).astype(bf16)
        return unused

    lax.fori_loop(0, PAIRS, pair_step, 0)


def attend(info, queries, held, got, meta):
    return pl.pallas_call(
        attend_kernel,
        out_shape=jax.ShapeDtypeStruct((GROUP, PIECE + STAT, HD), bf16),
        in_specs=[ANY] + [VMEM] * 6 + [ANY],
        out_specs=VMEM,
        scratch_shapes=[
            pltpu.SMEM((INFO,), i32),
            pltpu.VMEM((META, 128), f32),
            pltpu.SemaphoreType.DMA((2,)),
            pltpu.VMEM((KEYS, HD), bf16),
            pltpu.VMEM((KEYS, 2 * HD), bf16),
            pltpu.VMEM((PAIRS, PROWS, HD), bf16),
            pltpu.VMEM((STEPS, PROWS, CHUNK), f32),
            pltpu.VMEM((PROWS, 128), f32),
            pltpu.VMEM((PROWS, 2 * HD), f32),
        ],
        compiler_params=pltpu.CompilerParams(vmem_limit_bytes=48 * 1024 * 1024),
        cost_estimate=pl.CostEstimate(flops=4 * 8000000 * HD, bytes_accessed=4000000, transcendentals=8000000),
        name="attend",
    )(info, *queries, held, got, meta)


def combine_kernel(r_ref, out_ref):
    parts = []
    for i in range(GROUP):
        stat = r_ref[i, pl.ds(PIECE, STAT), :].astype(f32)
        parts.append(stat[0:4] + stat[4:8] + stat[8:12])
    best = functools.reduce(jnp.maximum, parts)
    weights = [jnp.exp2(part - best) for part in parts]
    total = functools.reduce(jnp.add, weights)
    inverse = 1.0 / total
    table = jnp.concatenate([w * inverse for w in weights] + [jnp.zeros((ROWS - GROUP * HEADS, ROWS), f32)], axis=0).T
    for h in range(HEADS):
        out = jnp.zeros((ROWS, HD), f32)
        for i in range(GROUP):
            at = i * HEADS + h
            out = out + table[:, at : at + 1] * r_ref[i, pl.ds(h * ROWS, ROWS), :].astype(f32)
        out_ref[:, h * HD : (h + 1) * HD] = out.astype(bf16)


def body(queries, new_keys, new_values, cache_keys, cache_values, q_request, block_request):
    axes = ("xh", "y", "zh", "z0", "xl", "core")
    where = [lax.axis_index(a) for a in axes]
    core, xl = where[5], where[4]
    coord = jnp.stack(where + [jnp.int32(0)] * 2).astype(i32)

    across = lax.ppermute(queries, "z0", [(0, 1), (1, 0)])
    new = jnp.where(core == 0, new_keys, new_values).reshape(2, 2, NEWK, HD)
    old = jnp.where(core == 0, cache_keys, cache_values).reshape(2, 2, OLDK, HD)
    both = jnp.concatenate([new, old], axis=2)
    both = jnp.where(xl == 0, both[0], both[1])
    slots = jnp.broadcast_to(both[None], (SRC // 2, 2, SLOT, HD)).reshape(SRC, SLOT, HD)
    slots, across = lax.optimization_barrier((slots, across))
    pair = jnp.concatenate([queries, across], axis=0)
    held = lax.all_to_all(slots, ("y", "zh", "z0"), 0, 0)
    shared = [pair] + [lax.ppermute(pair, ("xh", "xl"), [(i, i ^ d) for i in range(4)]) for d in range(1, 4)]
    meta, info = pl.pallas_call(
        prep_kernel,
        out_shape=(jax.ShapeDtypeStruct((META, 128), f32), jax.ShapeDtypeStruct((INFO,), i32)),
        in_specs=[SMEM, SMEM, VMEM],
        out_specs=(VMEM, SMEM),
        cost_estimate=pl.CostEstimate(flops=1000000, bytes_accessed=800000, transcendentals=0),
        name="prep",
    )(coord, block_request, q_request.reshape(ROWS, ROWS))
    held, meta, info, *shared = lax.optimization_barrier((held, meta, info, *shared))
    got = lax.ppermute(held, "core", [(0, 1), (1, 0)])
    partial = attend(info, shared, held, got, meta)
    parts = lax.all_to_all(partial, ("xh", "z0", "xl"), 0, 0)
    return pl.pallas_call(
        combine_kernel,
        out_shape=jax.ShapeDtypeStruct((ROWS, HEADS * HD), bf16),
        in_specs=[VMEM],
        out_specs=VMEM,
        compiler_params=pltpu.CompilerParams(vmem_limit_bytes=16 * 1024 * 1024),
        name="combine",
    )(parts)


def solution(mesh):
    fine = Mesh(mesh.devices.reshape(2, 8, 4, 2, 2, 2), ("xh", "y", "zh", "z0", "xl", "core"))
    ctx, head = ("xh", "y", "zh", "z0"), ("xl", "core")
    return jax.shard_map(
        body,
        mesh=fine,
        in_specs=(P(ctx, head), P(ctx, None), P(ctx, None), P(ctx, None), P(ctx, None), P(), P()),
        out_specs=P(ctx, head),
        check_vma=False,
    )
```

```python
import functools
import math

import jax
import jax.numpy as jnp
from jax import lax
from jax.experimental import pallas as pl
from jax.experimental.pallas import tpu as pltpu
from jax.sharding import Mesh, PartitionSpec as P

HD = 128
BLK = 16
ROWS = 128
HEADS = 4
SRC = 64
NEWK = 32
OLDK = 16
PER = OLDK // BLK
SLOT = NEWK + OLDK
GROUP = 8
TBS = 4
PAIRS = TBS // 2
SUB1, SUB2 = 256, 256
UNITS = 4
CHUNK = 256
NEW0 = SRC * OLDK + CHUNK
KEYS = NEW0 + SRC * NEWK + CHUNK
STEPS = (SRC * OLDK + SRC * NEWK) // CHUNK
LOW = -1.0e30
SCALE2 = math.log2(math.e) / math.sqrt(HD)
PIECE = HEADS * ROWS
PROWS = 4 * PIECE
STAT = 16
LO0, HI0, CODE0 = 0, TBS * ROWS, 2 * TBS * ROWS
META = CODE0 + (KEYS // 128 + 7) // 8 * 8
BLOCKS = SRC * PER
TB0, INFO = BLOCKS, BLOCKS + 4 * PAIRS

f32, bf16, i32 = jnp.float32, jnp.bfloat16, jnp.int32
VMEM = pl.BlockSpec(memory_space=pltpu.VMEM)
SMEM = pl.BlockSpec(memory_space=pltpu.SMEM)
HBM = pl.BlockSpec(memory_space=pltpu.HBM)


def pick(index, values):
    out = values[-1]
    for at in range(len(values) - 2, -1, -1):
        out = jnp.where(index == at, values[at], out)
    return out


def slots_kernel(new_keys, new_values, cache_keys, cache_values, slots):
    xl, core = lax.axis_index("xl"), lax.axis_index("core")

    def write(new, old):
        for z0 in range(2):
            part = xl * 2 + z0
            fresh = new[pl.ds(pl.multiple_of(part * NEWK, NEWK), NEWK), :]
            cached = old[pl.ds(pl.multiple_of(part * OLDK, OLDK), OLDK), :]
            for i in range(z0, SRC, 2):
                slots[i, :NEWK, :] = fresh
                slots[i, NEWK:, :] = cached

    @pl.when(core == 0)
    def _():
        write(new_keys, cache_keys)

    @pl.when(core == 1)
    def _():
        write(new_values, cache_values)


def prep_kernel(blocks, requests, meta, info):
    xh, y, zh, z0, xl = (lax.axis_index(a) for a in ("xh", "y", "zh", "z0", "xl"))
    part = xl * 2 + z0
    req = requests[...]
    starts = [jnp.int32(0)] + [
        jnp.sum(jnp.where(req < r, 1.0, 0.0).astype(f32)).astype(i32) for r in (1, 2, 3)
    ]

    def count(i, carry):
        r = blocks[(xh * SRC + i // PER) * 4 + part * PER + i % PER]
        return tuple(c + jnp.where(r == k, 1, 0) for k, c in enumerate(carry))

    zero = jnp.int32(0)
    n = lax.fori_loop(0, BLOCKS, count, (zero,) * 4)
    offs = [zero, n[0], n[0] + n[1], n[0] + n[1] + n[2], jnp.int32(BLOCKS)]

    def place(i, carry):
        r = blocks[(xh * SRC + i // PER) * 4 + part * PER + i % PER]
        info[i] = pick(r, carry)
        return tuple(c + jnp.where(r == k, 1, 0) for k, c in enumerate(carry))

    lax.fori_loop(0, BLOCKS, place, tuple(offs[:4]))

    lane = lax.broadcasted_iota(i32, (1, ROWS), 1)
    for pair in range(PAIRS):
        firsts, lasts = [], []
        for e in range(2):
            tb, own = pair * 2 + e, pair * SRC + y * 8 + zh * 2 + e
            row = requests[pl.ds(own, 1), :]
            rowf = row.astype(f32)
            firsts.append(jnp.min(rowf).astype(i32))
            lasts.append(jnp.max(rowf).astype(i32))
            lo = 2 * pick(row, starts)
            hi = 2 * (own * ROWS + lane) + 1
            meta[pl.ds(LO0 + tb * ROWS, ROWS), :] = jnp.broadcast_to(lo.astype(f32), (ROWS, ROWS)).T
            meta[pl.ds(HI0 + tb * ROWS, ROWS), :] = jnp.broadcast_to(hi.astype(f32), (ROWS, ROWS)).T
        first, last = firsts[0], lasts[1]
        clo = pick(first, offs[:4]) * BLK
        chi = pick(last, offs[1:]) * BLK
        cs = (clo >> 7) << 7
        info[TB0 + pair * 4 + 0] = cs
        info[TB0 + pair * 4 + 1] = jnp.where(chi > clo, (chi - cs + CHUNK - 1) // CHUNK, 0)
        base = xh * SRC
        a = jnp.maximum(pick(first, starts) >> 7, base)
        b = jnp.minimum(own, base + SRC - 1)
        ns = (((a - base) * NEWK) >> 7) << 7
        end = (b - base + 1) * NEWK
        info[TB0 + pair * 4 + 2] = NEW0 + ns
        info[TB0 + pair * 4 + 3] = jnp.where(a <= b, (end - ns + CHUNK - 1) // CHUNK, 0)

    shape = (META - CODE0, 128)
    key = lax.broadcasted_iota(i32, shape, 0) * 128 + lax.broadcasted_iota(i32, shape, 1)
    block = key >> 4
    cached = jnp.where(
        block >= offs[3],
        starts[3],
        jnp.where(block >= offs[2], starts[2], jnp.where(block >= offs[1], starts[1], 0)),
    )
    u = key - NEW0
    fresh = ROWS * (xh * SRC + (u >> 5)) + NEWK * part + (u & (NEWK - 1))
    code = jnp.where(key < SRC * OLDK, 2 * cached, -1)
    code = jnp.where((u >= 0) & (u < SRC * NEWK), 2 * fresh + 1, code)
    meta[pl.ds(CODE0, META - CODE0), :] = code.astype(f32)


def attend_kernel(info_in, *refs):
    q_refs, refs = refs[:4], refs[4:]
    own_ref, got_ref, meta_in, o_ref, info, meta, sem, kbuf, vbuf, qs, ss, mx, acc = refs
    copy_info = pltpu.make_async_copy(info_in, info, sem.at[0])
    copy_meta = pltpu.make_async_copy(meta_in, meta, sem.at[1])
    copy_info.start()
    copy_meta.start()
    for at in (SRC * OLDK, KEYS - CHUNK):
        kbuf[pl.ds(at, CHUNK), :] = jnp.zeros((CHUNK, HD), bf16)
        vbuf[pl.ds(at, CHUNK), :HD] = jnp.zeros((CHUNK, HD), bf16)
    vbuf[:, HD:] = jnp.ones((KEYS, HD), bf16)
    xh, z0, xl, core = (lax.axis_index(a) for a in ("xh", "z0", "xl", "core"))
    for d in range(4):
        for e in range(2):
            for h in range(HEADS):
                at = pl.multiple_of(((z0 ^ e) * 2 + (xl ^ (d & 1))) * PIECE + h * ROWS, ROWS)
                qs[xh ^ (d >> 1), pl.ds(at, ROWS), :] = q_refs[d][pl.ds(e * ROWS, ROWS), h * HD : (h + 1) * HD]

    copy_info.wait()

    def fill(buf, ref):
        buf[pl.ds(NEW0, SRC * NEWK), :HD] = ref[:, :NEWK, :].reshape(SRC * NEWK, HD)
        for i in range(BLOCKS):
            to = pl.multiple_of(info[i] * BLK, BLK)
            buf[pl.ds(to, BLK), :HD] = ref[i // PER, pl.ds(NEWK + (i % PER) * BLK, BLK), :]

    @pl.when(core == 0)
    def _():
        fill(kbuf, own_ref)
        fill(vbuf, got_ref)

    @pl.when(core == 1)
    def _():
        fill(kbuf, got_ref)
        fill(vbuf, own_ref)

    lane = lax.broadcasted_iota(i32, (ROWS, ROWS), 1)
    heads = range(4 * HEADS)
    copy_meta.wait()

    def pair_step(pair, unused):
        mx[...] = jnp.full(mx.shape, LOW, f32)
        acc[...] = jnp.zeros(acc.shape, f32)
        cs, nc, ns, nn = (info[TB0 + pair * 4 + i] for i in range(4))

        def place(j):
            return pl.multiple_of(jnp.where(j < nc, cs + j * CHUNK, ns + (j - nc) * CHUNK), 128)

        def score_step(j, units):
            keys, bias = [], ([], [])
            for i in range(units):
                at = place(j + i)
                keys.append(kbuf[pl.ds(at, CHUNK), :])
                for g in range(CHUNK // 128):
                    code = meta[pl.ds(CODE0 + (at >> 7) + g, 1), :]
                    for e in range(2):
                        line = (pair * 2 + e) * ROWS
                        lo = meta[pl.ds(pl.multiple_of(LO0 + line, ROWS), ROWS), :]
                        hi = meta[pl.ds(pl.multiple_of(HI0 + line, ROWS), ROWS), :]
                        bias[e].append(jnp.where((code >= lo) & (code <= hi), 0.0, LOW))
            keys = jnp.concatenate(keys, axis=0)
            for h in heads:
                low = h * ROWS % SUB1
                if low == 0:
                    s = lax.dot_general(
                        qs[pair, pl.ds(h * ROWS, SUB1), :], keys, (((1,), (1,)), ((), ())), preferred_element_type=f32
                    )
                rows = pl.ds(h * ROWS, ROWS)
                best = mx[rows, :]
                for g in range(units * CHUNK // 128):
                    part = s[low : low + ROWS, g * 128 : (g + 1) * 128] * SCALE2 + bias[h // 8][g]
                    ss[j + g // 2, rows, (g % 2) * 128 : (g % 2 + 1) * 128] = part
                    best = jnp.maximum(best, part)
                mx[rows, :] = best

        def sweep(step):
            n = nc + nn

            def most(i, unused):
                step(i * UNITS, UNITS)
                return unused

            lax.fori_loop(0, n // UNITS, most, 0)
            units = UNITS // 2
            while units:
                left = n % (2 * units)

                @pl.when(left >= units)
                def _(units=units, left=left):
                    step(n - left, units)

                units //= 2

        sweep(score_step)
        for h in heads:
            rows = pl.ds(h * ROWS, ROWS)
            mx[rows, :] = jnp.broadcast_to(jnp.max(mx[rows, :], axis=1, keepdims=True), (ROWS, 128))

        def value_step(j, units):
            v = jnp.concatenate([vbuf[pl.ds(place(j + i), CHUNK), :] for i in range(units)], axis=0)
            probs = []
            for h in heads:
                rows = pl.ds(h * ROWS, ROWS)
                best = mx[rows, :]
                parts = []
                for g in range(units * CHUNK // 128):
                    p = jnp.exp2(ss[j + g // 2, rows, (g % 2) * 128 : (g % 2 + 1) * 128] - best)
                    parts.append(p.astype(bf16))
                probs.append(jnp.concatenate(parts, axis=1))
                if len(probs) * ROWS == SUB2:
                    acc[pl.ds((h + 1) * ROWS - SUB2, SUB2), :] += lax.dot_general(
                        jnp.concatenate(probs, axis=0), v, (((1,), (0,)), ((), ())), preferred_element_type=f32
                    )
                    probs = []

        sweep(value_step)
        best, sums = jnp.zeros((ROWS, ROWS), f32), jnp.ones((ROWS, ROWS), f32)
        for h in heads:
            rows = pl.ds(h * ROWS, ROWS)
            total = acc[rows, HD:]
            total = jnp.where(total > 0.0, total, 1.0)
            inverse = pl.reciprocal(total, approx=True)
            inverse = inverse * (2.0 - total * inverse)
            o_ref[pair * 4 + h // HEADS, pl.ds((h % HEADS) * ROWS, ROWS), :] = (acc[rows, :HD] * inverse).astype(bf16)
            best = jnp.where(lane == h, mx[rows, :], best)
            sums = jnp.where(lane == h, total, sums)
        stat = (best + jnp.log2(sums)).T
        for i in range(4):
            part = stat[i * HEADS : (i + 1) * HEADS]
            top = part.astype(bf16)
            rest = part - top.astype(f32)
            mid = rest.astype(bf16)
            low = (rest - mid.astype(f32)).astype(bf16)
            o_ref[pair * 4 + i, pl.ds(PIECE, STAT), :] = jnp.concatenate(
                [top.astype(f32), mid.astype(f32), low.astype(f32), jnp.zeros((HEADS, ROWS), f32)], axis=0
            ).astype(bf16)
        return unused

    lax.fori_loop(0, PAIRS, pair_step, 0)


def attend(info, queries, held, got, meta):
    return pl.pallas_call(
        attend_kernel,
        out_shape=jax.ShapeDtypeStruct((GROUP, PIECE + STAT, HD), bf16),
        in_specs=[HBM] + [VMEM] * 6 + [HBM],
        out_specs=VMEM,
        scratch_shapes=[
            pltpu.SMEM((INFO,), i32),
            pltpu.VMEM((META, 128), f32),
            pltpu.SemaphoreType.DMA((2,)),
            pltpu.VMEM((KEYS, HD), bf16),
            pltpu.VMEM((KEYS, 2 * HD), bf16),
            pltpu.VMEM((PAIRS, PROWS, HD), bf16),
            pltpu.VMEM((STEPS, PROWS, CHUNK), f32),
            pltpu.VMEM((PROWS, 128), f32),
            pltpu.VMEM((PROWS, 2 * HD), f32),
        ],
        compiler_params=pltpu.CompilerParams(vmem_limit_bytes=48 * 1024 * 1024),
        cost_estimate=pl.CostEstimate(flops=4 * 8000000 * HD, bytes_accessed=4000000, transcendentals=8000000),
        name="attend",
    )(info, *queries, held, got, meta)


def combine_kernel(r_ref, out_ref):
    parts = []
    for i in range(GROUP):
        stat = r_ref[i, pl.ds(PIECE, STAT), :].astype(f32)
        parts.append(stat[0:4] + stat[4:8] + stat[8:12])
    best = functools.reduce(jnp.maximum, parts)
    weights = [jnp.exp2(part - best) for part in parts]
    total = functools.reduce(jnp.add, weights)
    inverse = 1.0 / total
    table = jnp.concatenate([w * inverse for w in weights] + [jnp.zeros((ROWS - GROUP * HEADS, ROWS), f32)], axis=0).T
    for h in range(HEADS):
        out = jnp.zeros((ROWS, HD), f32)
        for i in range(GROUP):
            at = i * HEADS + h
            out = out + table[:, at : at + 1] * r_ref[i, pl.ds(h * ROWS, ROWS), :].astype(f32)
        out_ref[:, h * HD : (h + 1) * HD] = out.astype(bf16)


def body(queries, new_keys, new_values, cache_keys, cache_values, q_request, block_request):
    across = lax.ppermute(queries, "z0", [(0, 1), (1, 0)])
    slots = pl.pallas_call(
        slots_kernel,
        out_shape=jax.ShapeDtypeStruct((SRC, SLOT, HD), bf16),
        in_specs=[VMEM] * 4,
        out_specs=VMEM,
        cost_estimate=pl.CostEstimate(flops=1000000, bytes_accessed=4000000, transcendentals=0),
        name="slots",
    )(new_keys, new_values, cache_keys, cache_values)
    slots, across = lax.optimization_barrier((slots, across))
    pair = jnp.concatenate([queries, across], axis=0)
    held = lax.all_to_all(slots, ("y", "zh", "z0"), 0, 0)
    shared = [pair] + [lax.ppermute(pair, ("xh", "xl"), [(i, i ^ d) for i in range(4)]) for d in range(1, 4)]
    meta, info = pl.pallas_call(
        prep_kernel,
        out_shape=(jax.ShapeDtypeStruct((META, 128), f32), jax.ShapeDtypeStruct((INFO,), i32)),
        in_specs=[SMEM, VMEM],
        out_specs=(VMEM, SMEM),
        cost_estimate=pl.CostEstimate(flops=1000000, bytes_accessed=800000, transcendentals=0),
        compiler_params=pltpu.CompilerParams(vmem_limit_bytes=8 * 1024 * 1024),
        name="prep",
    )(block_request, q_request.reshape(ROWS, ROWS))
    held, meta, info, *shared = lax.optimization_barrier((held, meta, info, *shared))
    got = lax.ppermute(held, "core", [(0, 1), (1, 0)])
    partial = attend(info, shared, held, got, meta)
    parts = lax.all_to_all(partial, ("xh", "z0", "xl"), 0, 0)
    return pl.pallas_call(
        combine_kernel,
        out_shape=jax.ShapeDtypeStruct((ROWS, HEADS * HD), bf16),
        in_specs=[VMEM],
        out_specs=VMEM,
        compiler_params=pltpu.CompilerParams(vmem_limit_bytes=16 * 1024 * 1024),
        name="combine",
    )(parts)


def solution(mesh):
    fine = Mesh(mesh.devices.reshape(2, 8, 4, 2, 2, 2), ("xh", "y", "zh", "z0", "xl", "core"))
    ctx, head = ("xh", "y", "zh", "z0"), ("xl", "core")
    return jax.shard_map(
        body,
        mesh=fine,
        in_specs=(P(ctx, head), P(ctx, None), P(ctx, None), P(ctx, None), P(ctx, None), P(), P()),
        out_specs=P(ctx, head),
        check_vma=False,
    )
```

```python
import functools
import math

import jax
import jax.numpy as jnp
from jax import lax
from jax.experimental import pallas as pl
from jax.experimental.pallas import tpu as pltpu
from jax.sharding import Mesh, PartitionSpec as P

HD = 128
BLK = 16
ROWS = 128
HEADS = 4
SRC = 64
NEWK = 32
OLDK = 16
PER = OLDK // BLK
SLOT = NEWK + OLDK
GROUP = 8
TBS = 4
PAIRS = TBS // 2
SUB1, SUB2 = 256, 256
UNITS = 4
CHUNK = 256
NEW0 = SRC * OLDK + CHUNK
KEYS = NEW0 + SRC * NEWK + CHUNK
STEPS = (SRC * OLDK + SRC * NEWK) // CHUNK
LOW = -1.0e30
SCALE2 = math.log2(math.e) / math.sqrt(HD)
PIECE = HEADS * ROWS
PROWS = 4 * PIECE
STAT = 16
LO0, HI0, CODE0 = 0, TBS * ROWS, 2 * TBS * ROWS
META = CODE0 + (KEYS // 128 + 7) // 8 * 8
BLOCKS = SRC * PER
TB0, INFO = BLOCKS, BLOCKS + 4 * PAIRS

f32, bf16, i32 = jnp.float32, jnp.bfloat16, jnp.int32
VMEM = pl.BlockSpec(memory_space=pltpu.VMEM)
SMEM = pl.BlockSpec(memory_space=pltpu.SMEM)
HBM = pl.BlockSpec(memory_space=pltpu.HBM)


def pick(index, values):
    out = values[-1]
    for at in range(len(values) - 2, -1, -1):
        out = jnp.where(index == at, values[at], out)
    return out


def slots_kernel(new_keys, new_values, cache_keys, cache_values, slots):
    xl, core = lax.axis_index("xl"), lax.axis_index("core")

    def write(new, old):
        for z0 in range(2):
            part = xl * 2 + z0
            fresh = new[pl.ds(pl.multiple_of(part * NEWK, NEWK), NEWK), :]
            cached = old[pl.ds(pl.multiple_of(part * OLDK, OLDK), OLDK), :]
            for i in range(z0, SRC, 2):
                slots[i, :NEWK, :] = fresh
                slots[i, NEWK:, :] = cached

    @pl.when(core == 0)
    def _():
        write(new_keys, cache_keys)

    @pl.when(core == 1)
    def _():
        write(new_values, cache_values)


def prep_kernel(blocks, requests, meta, info):
    xh, y, zh, z0, xl = (lax.axis_index(a) for a in ("xh", "y", "zh", "z0", "xl"))
    part = xl * 2 + z0
    req = requests[...]
    starts = [jnp.int32(0)] + [
        jnp.sum(jnp.where(req < r, 1.0, 0.0).astype(f32)).astype(i32) for r in (1, 2, 3)
    ]

    def count(i, carry):
        r = blocks[(xh * SRC + i // PER) * 4 + part * PER + i % PER]
        return tuple(c + jnp.where(r == k, 1, 0) for k, c in enumerate(carry))

    zero = jnp.int32(0)
    n = lax.fori_loop(0, BLOCKS, count, (zero,) * 4)
    offs = [zero, n[0], n[0] + n[1], n[0] + n[1] + n[2], jnp.int32(BLOCKS)]

    def place(i, carry):
        r = blocks[(xh * SRC + i // PER) * 4 + part * PER + i % PER]
        info[i] = pick(r, carry)
        return tuple(c + jnp.where(r == k, 1, 0) for k, c in enumerate(carry))

    lax.fori_loop(0, BLOCKS, place, tuple(offs[:4]))

    lane = lax.broadcasted_iota(i32, (1, ROWS), 1)
    for pair in range(PAIRS):
        firsts, lasts = [], []
        for e in range(2):
            tb, own = pair * 2 + e, pair * SRC + y * 8 + zh * 2 + e
            row = requests[pl.ds(own, 1), :]
            rowf = row.astype(f32)
            firsts.append(jnp.min(rowf).astype(i32))
            lasts.append(jnp.max(rowf).astype(i32))
            lo = 2 * pick(row, starts)
            hi = 2 * (own * ROWS + lane) + 1
            meta[pl.ds(LO0 + tb * ROWS, ROWS), :] = jnp.broadcast_to(lo.astype(f32), (ROWS, ROWS)).T
            meta[pl.ds(HI0 + tb * ROWS, ROWS), :] = jnp.broadcast_to(hi.astype(f32), (ROWS, ROWS)).T
        first, last = firsts[0], lasts[1]
        clo = pick(first, offs[:4]) * BLK
        chi = pick(last, offs[1:]) * BLK
        cs = (clo >> 7) << 7
        info[TB0 + pair * 4 + 0] = cs
        info[TB0 + pair * 4 + 1] = jnp.where(chi > clo, (chi - cs + CHUNK - 1) // CHUNK, 0)
        base = xh * SRC
        a = jnp.maximum(pick(first, starts) >> 7, base)
        b = jnp.minimum(own, base + SRC - 1)
        ns = (((a - base) * NEWK) >> 7) << 7
        end = (b - base + 1) * NEWK
        info[TB0 + pair * 4 + 2] = NEW0 + ns
        info[TB0 + pair * 4 + 3] = jnp.where(a <= b, (end - ns + CHUNK - 1) // CHUNK, 0)

    shape = (META - CODE0, 128)
    key = lax.broadcasted_iota(i32, shape, 0) * 128 + lax.broadcasted_iota(i32, shape, 1)
    block = key >> 4
    cached = jnp.where(
        block >= offs[3],
        starts[3],
        jnp.where(block >= offs[2], starts[2], jnp.where(block >= offs[1], starts[1], 0)),
    )
    u = key - NEW0
    fresh = ROWS * (xh * SRC + (u >> 5)) + NEWK * part + (u & (NEWK - 1))
    code = jnp.where(key < SRC * OLDK, 2 * cached, -1)
    code = jnp.where((u >= 0) & (u < SRC * NEWK), 2 * fresh + 1, code)
    meta[pl.ds(CODE0, META - CODE0), :] = code.astype(f32)


def attend_kernel(info_in, *refs):
    q_refs, refs = refs[:4], refs[4:]
    own_ref, got_ref, meta_in, o_ref, info, meta, sem, kbuf, vbuf, qs, ss, mx, acc = refs
    copy_info = pltpu.make_async_copy(info_in, info, sem.at[0])
    copy_meta = pltpu.make_async_copy(meta_in, meta, sem.at[1])
    copy_info.start()
    copy_meta.start()
    for at in (SRC * OLDK, KEYS - CHUNK):
        kbuf[pl.ds(at, CHUNK), :] = jnp.zeros((CHUNK, HD), bf16)
        vbuf[pl.ds(at, CHUNK), :HD] = jnp.zeros((CHUNK, HD), bf16)
    vbuf[:, HD:] = jnp.ones((KEYS, HD), bf16)
    xh, z0, xl, core = (lax.axis_index(a) for a in ("xh", "z0", "xl", "core"))
    for d in range(4):
        for e in range(2):
            for h in range(HEADS):
                at = pl.multiple_of(((z0 ^ e) * 2 + (xl ^ (d & 1))) * PIECE + h * ROWS, ROWS)
                qs[xh ^ (d >> 1), pl.ds(at, ROWS), :] = q_refs[d][pl.ds(e * ROWS, ROWS), h * HD : (h + 1) * HD]

    copy_info.wait()

    def fill(buf, ref):
        buf[pl.ds(NEW0, SRC * NEWK), :HD] = ref[:, :NEWK, :].reshape(SRC * NEWK, HD)
        for i in range(BLOCKS):
            to = pl.multiple_of(info[i] * BLK, BLK)
            buf[pl.ds(to, BLK), :HD] = ref[i // PER, pl.ds(NEWK + (i % PER) * BLK, BLK), :]

    @pl.when(core == 0)
    def _():
        fill(kbuf, own_ref)
        fill(vbuf, got_ref)

    @pl.when(core == 1)
    def _():
        fill(kbuf, got_ref)
        fill(vbuf, own_ref)

    lane = lax.broadcasted_iota(i32, (ROWS, ROWS), 1)
    heads = range(4 * HEADS)
    copy_meta.wait()

    def pair_step(pair, unused):
        mx[...] = jnp.full(mx.shape, LOW, f32)
        acc[...] = jnp.zeros(acc.shape, f32)
        cs, nc, ns, nn = (info[TB0 + pair * 4 + i] for i in range(4))

        def place(j):
            return pl.multiple_of(jnp.where(j < nc, cs + j * CHUNK, ns + (j - nc) * CHUNK), 128)

        def score_step(j, units):
            keys, bias = [], ([], [])
            for i in range(units):
                at = place(j + i)
                keys.append(kbuf[pl.ds(at, CHUNK), :])
                for g in range(CHUNK // 128):
                    code = meta[pl.ds(CODE0 + (at >> 7) + g, 1), :]
                    for e in range(2):
                        line = (pair * 2 + e) * ROWS
                        lo = meta[pl.ds(pl.multiple_of(LO0 + line, ROWS), ROWS), :]
                        hi = meta[pl.ds(pl.multiple_of(HI0 + line, ROWS), ROWS), :]
                        bias[e].append(jnp.where((code >= lo) & (code <= hi), 0.0, LOW))
            keys = jnp.concatenate(keys, axis=0)
            for h in heads:
                low = h * ROWS % SUB1
                if low == 0:
                    s = lax.dot_general(
                        qs[pair, pl.ds(h * ROWS, SUB1), :], keys, (((1,), (1,)), ((), ())), preferred_element_type=f32
                    )
                rows = pl.ds(h * ROWS, ROWS)
                best = mx[rows, :]
                for g in range(units * CHUNK // 128):
                    part = s[low : low + ROWS, g * 128 : (g + 1) * 128] * SCALE2 + bias[h // 8][g]
                    ss[j + g // 2, rows, (g % 2) * 128 : (g % 2 + 1) * 128] = part
                    best = jnp.maximum(best, part)
                mx[rows, :] = best

        def sweep(step):
            n = nc + nn

            def most(i, unused):
                step(i * UNITS, UNITS)
                return unused

            lax.fori_loop(0, n // UNITS, most, 0)
            units = UNITS // 2
            while units:
                left = n % (2 * units)

                @pl.when(left >= units)
                def _(units=units, left=left):
                    step(n - left, units)

                units //= 2

        sweep(score_step)
        for h in heads:
            rows = pl.ds(h * ROWS, ROWS)
            mx[rows, :] = jnp.broadcast_to(jnp.max(mx[rows, :], axis=1, keepdims=True), (ROWS, 128))

        def value_step(j, units):
            v = jnp.concatenate([vbuf[pl.ds(place(j + i), CHUNK), :] for i in range(units)], axis=0)
            probs = []
            for h in heads:
                rows = pl.ds(h * ROWS, ROWS)
                best = mx[rows, :]
                parts = []
                for g in range(units * CHUNK // 128):
                    p = jnp.exp2(ss[j + g // 2, rows, (g % 2) * 128 : (g % 2 + 1) * 128] - best)
                    parts.append(p.astype(bf16))
                probs.append(jnp.concatenate(parts, axis=1))
                if len(probs) * ROWS == SUB2:
                    acc[pl.ds((h + 1) * ROWS - SUB2, SUB2), :] += lax.dot_general(
                        jnp.concatenate(probs, axis=0), v, (((1,), (0,)), ((), ())), preferred_element_type=f32
                    )
                    probs = []

        sweep(value_step)
        best, sums = jnp.zeros((ROWS, ROWS), f32), jnp.ones((ROWS, ROWS), f32)
        for h in heads:
            rows = pl.ds(h * ROWS, ROWS)
            total = acc[rows, HD:]
            total = jnp.where(total > 0.0, total, 1.0)
            inverse = pl.reciprocal(total, approx=True)
            inverse = inverse * (2.0 - total * inverse)
            o_ref[pair * 4 + h // HEADS, pl.ds((h % HEADS) * ROWS, ROWS), :] = (acc[rows, :HD] * inverse).astype(bf16)
            best = jnp.where(lane == h, mx[rows, :], best)
            sums = jnp.where(lane == h, total, sums)
        stat = (best + jnp.log2(sums)).T
        for i in range(4):
            part = stat[i * HEADS : (i + 1) * HEADS]
            top = part.astype(bf16)
            rest = part - top.astype(f32)
            mid = rest.astype(bf16)
            low = (rest - mid.astype(f32)).astype(bf16)
            o_ref[pair * 4 + i, pl.ds(PIECE, STAT), :] = jnp.concatenate(
                [top.astype(f32), mid.astype(f32), low.astype(f32), jnp.zeros((HEADS, ROWS), f32)], axis=0
            ).astype(bf16)
        return unused

    lax.fori_loop(0, PAIRS, pair_step, 0)


def attend(info, queries, held, got, meta):
    return pl.pallas_call(
        attend_kernel,
        out_shape=jax.ShapeDtypeStruct((GROUP, PIECE + STAT, HD), bf16),
        in_specs=[HBM] + [VMEM] * 6 + [HBM],
        out_specs=VMEM,
        scratch_shapes=[
            pltpu.SMEM((INFO,), i32),
            pltpu.VMEM((META, 128), f32),
            pltpu.SemaphoreType.DMA((2,)),
            pltpu.VMEM((KEYS, HD), bf16),
            pltpu.VMEM((KEYS, 2 * HD), bf16),
            pltpu.VMEM((PAIRS, PROWS, HD), bf16),
            pltpu.VMEM((STEPS, PROWS, CHUNK), f32),
            pltpu.VMEM((PROWS, 128), f32),
            pltpu.VMEM((PROWS, 2 * HD), f32),
        ],
        compiler_params=pltpu.CompilerParams(vmem_limit_bytes=48 * 1024 * 1024),
        cost_estimate=pl.CostEstimate(flops=4 * 8000000 * HD, bytes_accessed=4000000, transcendentals=8000000),
        name="attend",
    )(info, *queries, held, got, meta)


def combine_kernel(r_ref, out_ref):
    parts = []
    for i in range(GROUP):
        stat = r_ref[i, pl.ds(PIECE, STAT), :].astype(f32)
        parts.append(stat[0:4] + stat[4:8] + stat[8:12])
    best = functools.reduce(jnp.maximum, parts)
    weights = [jnp.exp2(part - best) for part in parts]
    total = functools.reduce(jnp.add, weights)
    inverse = 1.0 / total
    table = jnp.concatenate([w * inverse for w in weights] + [jnp.zeros((ROWS - GROUP * HEADS, ROWS), f32)], axis=0).T
    for h in range(HEADS):
        out = jnp.zeros((ROWS, HD), f32)
        for i in range(GROUP):
            at = i * HEADS + h
            out = out + table[:, at : at + 1] * r_ref[i, pl.ds(h * ROWS, ROWS), :].astype(f32)
        out_ref[:, h * HD : (h + 1) * HD] = out.astype(bf16)


def body(queries, new_keys, new_values, cache_keys, cache_values, q_request, block_request):
    across = lax.ppermute(queries, "z0", [(0, 1), (1, 0)])
    slots = pl.pallas_call(
        slots_kernel,
        out_shape=jax.ShapeDtypeStruct((SRC, SLOT, HD), bf16),
        in_specs=[VMEM] * 4,
        out_specs=VMEM,
        cost_estimate=pl.CostEstimate(flops=1000000, bytes_accessed=4000000, transcendentals=0),
        name="slots",
    )(new_keys, new_values, cache_keys, cache_values)
    pair = jnp.concatenate([queries, across], axis=0)
    held = lax.all_to_all(slots, ("y", "zh", "z0"), 0, 0)
    shared = [pair] + [lax.ppermute(pair, ("xh", "xl"), [(i, i ^ d) for i in range(4)]) for d in range(1, 4)]
    meta, info = pl.pallas_call(
        prep_kernel,
        out_shape=(jax.ShapeDtypeStruct((META, 128), f32), jax.ShapeDtypeStruct((INFO,), i32)),
        in_specs=[SMEM, VMEM],
        out_specs=(VMEM, SMEM),
        cost_estimate=pl.CostEstimate(flops=30000000000, bytes_accessed=800000, transcendentals=0),
        compiler_params=pltpu.CompilerParams(vmem_limit_bytes=8 * 1024 * 1024),
        name="prep",
    )(block_request, q_request.reshape(ROWS, ROWS))
    held, meta, info, *shared = lax.optimization_barrier((held, meta, info, *shared))
    got = lax.ppermute(held, "core", [(0, 1), (1, 0)])
    partial = attend(info, shared, held, got, meta)
    parts = lax.all_to_all(partial, ("xh", "z0", "xl"), 0, 0)
    return pl.pallas_call(
        combine_kernel,
        out_shape=jax.ShapeDtypeStruct((ROWS, HEADS * HD), bf16),
        in_specs=[VMEM],
        out_specs=VMEM,
        compiler_params=pltpu.CompilerParams(vmem_limit_bytes=16 * 1024 * 1024),
        name="combine",
    )(parts)


def solution(mesh):
    fine = Mesh(mesh.devices.reshape(2, 8, 4, 2, 2, 2), ("xh", "y", "zh", "z0", "xl", "core"))
    ctx, head = ("xh", "y", "zh", "z0"), ("xl", "core")
    return jax.shard_map(
        body,
        mesh=fine,
        in_specs=(P(ctx, head), P(ctx, None), P(ctx, None), P(ctx, None), P(ctx, None), P(), P()),
        out_specs=P(ctx, head),
        check_vma=False,
    )
```

```python
import functools
import math

import jax
import jax.numpy as jnp
from jax import lax
from jax.experimental import pallas as pl
from jax.experimental.pallas import tpu as pltpu
from jax.sharding import Mesh, PartitionSpec as P

HD = 128
BLK = 16
ROWS = 128
HEADS = 4
SRC = 64
NEWK = 32
OLDK = 16
PER = OLDK // BLK
SLOT = NEWK + OLDK
GROUP = 8
TBS = 4
PAIRS = TBS // 2
SUB1, SUB2 = 256, 256
UNITS = 4
CHUNK = 256
NEW0 = SRC * OLDK + CHUNK
KEYS = NEW0 + SRC * NEWK + CHUNK
STEPS = (SRC * OLDK + SRC * NEWK) // CHUNK
LOW = -1.0e30
SCALE2 = math.log2(math.e) / math.sqrt(HD)
PIECE = HEADS * ROWS
PROWS = 4 * PIECE
STAT = 16
LO0, HI0, CODE0 = 0, TBS * ROWS, 2 * TBS * ROWS
META = CODE0 + (KEYS // 128 + 7) // 8 * 8
BLOCKS = SRC * PER
TB0, INFO = BLOCKS, BLOCKS + 4 * PAIRS

f32, bf16, i32 = jnp.float32, jnp.bfloat16, jnp.int32
VMEM = pl.BlockSpec(memory_space=pltpu.VMEM)
SMEM = pl.BlockSpec(memory_space=pltpu.SMEM)
HBM = pl.BlockSpec(memory_space=pltpu.HBM)


def pick(index, values):
    out = values[-1]
    for at in range(len(values) - 2, -1, -1):
        out = jnp.where(index == at, values[at], out)
    return out


def slots_kernel(new_keys, new_values, cache_keys, cache_values, slots):
    xl, core = lax.axis_index("xl"), lax.axis_index("core")

    def write(new, old):
        for z0 in range(2):
            part = xl * 2 + z0
            fresh = new[pl.ds(pl.multiple_of(part * NEWK, NEWK), NEWK), :]
            cached = old[pl.ds(pl.multiple_of(part * OLDK, OLDK), OLDK), :]
            for i in range(z0, SRC, 2):
                slots[i, :NEWK, :] = fresh
                slots[i, NEWK:, :] = cached

    @pl.when(core == 0)
    def _():
        write(new_keys, cache_keys)

    @pl.when(core == 1)
    def _():
        write(new_values, cache_values)


def prep_kernel(blocks, requests, meta, info):
    xh, y, zh, z0, xl = (lax.axis_index(a) for a in ("xh", "y", "zh", "z0", "xl"))
    part = xl * 2 + z0
    req = requests[...]
    starts = [jnp.int32(0)] + [
        jnp.sum(jnp.where(req < r, 1.0, 0.0).astype(f32)).astype(i32) for r in (1, 2, 3)
    ]

    def count(i, carry):
        r = blocks[(xh * SRC + i // PER) * 4 + part * PER + i % PER]
        return tuple(c + jnp.where(r == k, 1, 0) for k, c in enumerate(carry))

    zero = jnp.int32(0)
    n = lax.fori_loop(0, BLOCKS, count, (zero,) * 4)
    offs = [zero, n[0], n[0] + n[1], n[0] + n[1] + n[2], jnp.int32(BLOCKS)]

    def place(i, carry):
        r = blocks[(xh * SRC + i // PER) * 4 + part * PER + i % PER]
        info[i] = pick(r, carry)
        return tuple(c + jnp.where(r == k, 1, 0) for k, c in enumerate(carry))

    lax.fori_loop(0, BLOCKS, place, tuple(offs[:4]))

    lane = lax.broadcasted_iota(i32, (1, ROWS), 1)
    for pair in range(PAIRS):
        firsts, lasts = [], []
        for e in range(2):
            tb, own = pair * 2 + e, pair * SRC + y * 8 + zh * 2 + e
            row = requests[pl.ds(own, 1), :]
            rowf = row.astype(f32)
            firsts.append(jnp.min(rowf).astype(i32))
            lasts.append(jnp.max(rowf).astype(i32))
            lo = 2 * pick(row, starts)
            hi = 2 * (own * ROWS + lane) + 1
            meta[pl.ds(LO0 + tb * ROWS, ROWS), :] = jnp.broadcast_to(lo.astype(f32), (ROWS, ROWS)).T
            meta[pl.ds(HI0 + tb * ROWS, ROWS), :] = jnp.broadcast_to(hi.astype(f32), (ROWS, ROWS)).T
        first, last = firsts[0], lasts[1]
        clo = pick(first, offs[:4]) * BLK
        chi = pick(last, offs[1:]) * BLK
        cs = (clo >> 7) << 7
        info[TB0 + pair * 4 + 0] = cs
        info[TB0 + pair * 4 + 1] = jnp.where(chi > clo, (chi - cs + CHUNK - 1) // CHUNK, 0)
        base = xh * SRC
        a = jnp.maximum(pick(first, starts) >> 7, base)
        b = jnp.minimum(own, base + SRC - 1)
        ns = (((a - base) * NEWK) >> 7) << 7
        end = (b - base + 1) * NEWK
        info[TB0 + pair * 4 + 2] = NEW0 + ns
        info[TB0 + pair * 4 + 3] = jnp.where(a <= b, (end - ns + CHUNK - 1) // CHUNK, 0)

    shape = (META - CODE0, 128)
    key = lax.broadcasted_iota(i32, shape, 0) * 128 + lax.broadcasted_iota(i32, shape, 1)
    block = key >> 4
    cached = jnp.where(
        block >= offs[3],
        starts[3],
        jnp.where(block >= offs[2], starts[2], jnp.where(block >= offs[1], starts[1], 0)),
    )
    u = key - NEW0
    fresh = ROWS * (xh * SRC + (u >> 5)) + NEWK * part + (u & (NEWK - 1))
    code = jnp.where(key < SRC * OLDK, 2 * cached, -1)
    code = jnp.where((u >= 0) & (u < SRC * NEWK), 2 * fresh + 1, code)
    meta[pl.ds(CODE0, META - CODE0), :] = code.astype(f32)


def attend_kernel(info_in, *refs):
    q_refs, refs = refs[:4], refs[4:]
    own_ref, got_ref, meta_in, o_ref, info, meta, sem, kbuf, vbuf, qs, ss, mx, acc = refs
    copy_info = pltpu.make_async_copy(info_in, info, sem.at[0])
    copy_meta = pltpu.make_async_copy(meta_in, meta, sem.at[1])
    copy_info.start()
    copy_meta.start()
    for at in (SRC * OLDK, KEYS - CHUNK):
        kbuf[pl.ds(at, CHUNK), :] = jnp.zeros((CHUNK, HD), bf16)
        vbuf[pl.ds(at, CHUNK), :HD] = jnp.zeros((CHUNK, HD), bf16)
    vbuf[:, HD:] = jnp.ones((KEYS, HD), bf16)
    xh, z0, xl, core = (lax.axis_index(a) for a in ("xh", "z0", "xl", "core"))
    for d in range(4):
        for e in range(2):
            for h in range(HEADS):
                at = pl.multiple_of(((z0 ^ e) * 2 + (xl ^ (d & 1))) * PIECE + h * ROWS, ROWS)
                qs[xh ^ (d >> 1), pl.ds(at, ROWS), :] = q_refs[d][pl.ds(e * ROWS, ROWS), h * HD : (h + 1) * HD]

    copy_info.wait()

    def fill(buf, ref):
        buf[pl.ds(NEW0, SRC * NEWK), :HD] = ref[:, :NEWK, :].reshape(SRC * NEWK, HD)
        for i in range(BLOCKS):
            to = pl.multiple_of(info[i] * BLK, BLK)
            buf[pl.ds(to, BLK), :HD] = ref[i // PER, pl.ds(NEWK + (i % PER) * BLK, BLK), :]

    @pl.when(core == 0)
    def _():
        fill(kbuf, own_ref)
        fill(vbuf, got_ref)

    @pl.when(core == 1)
    def _():
        fill(kbuf, got_ref)
        fill(vbuf, own_ref)

    lane = lax.broadcasted_iota(i32, (ROWS, ROWS), 1)
    heads = range(4 * HEADS)
    copy_meta.wait()

    def pair_step(pair, unused):
        mx[...] = jnp.full(mx.shape, LOW, f32)
        acc[...] = jnp.zeros(acc.shape, f32)
        cs, nc, ns, nn = (info[TB0 + pair * 4 + i] for i in range(4))

        def place(j):
            return pl.multiple_of(jnp.where(j < nc, cs + j * CHUNK, ns + (j - nc) * CHUNK), 128)

        def score_step(j, units):
            keys, bias = [], ([], [])
            for i in range(units):
                at = place(j + i)
                keys.append(kbuf[pl.ds(at, CHUNK), :])
                for g in range(CHUNK // 128):
                    code = meta[pl.ds(CODE0 + (at >> 7) + g, 1), :]
                    for e in range(2):
                        line = (pair * 2 + e) * ROWS
                        lo = meta[pl.ds(pl.multiple_of(LO0 + line, ROWS), ROWS), :]
                        hi = meta[pl.ds(pl.multiple_of(HI0 + line, ROWS), ROWS), :]
                        bias[e].append(jnp.where((code >= lo) & (code <= hi), 0.0, LOW))
            keys = jnp.concatenate(keys, axis=0)
            for h in heads:
                low = h * ROWS % SUB1
                if low == 0:
                    s = lax.dot_general(
                        qs[pair, pl.ds(h * ROWS, SUB1), :], keys, (((1,), (1,)), ((), ())), preferred_element_type=f32
                    )
                rows = pl.ds(h * ROWS, ROWS)
                best = mx[rows, :]
                for g in range(units * CHUNK // 128):
                    part = s[low : low + ROWS, g * 128 : (g + 1) * 128] * SCALE2 + bias[h // 8][g]
                    ss[j + g // 2, rows, (g % 2) * 128 : (g % 2 + 1) * 128] = part
                    best = jnp.maximum(best, part)
                mx[rows, :] = best

        def sweep(step):
            n = nc + nn

            def most(i, unused):
                step(i * UNITS, UNITS)
                return unused

            lax.fori_loop(0, n // UNITS, most, 0)
            units = UNITS // 2
            while units:
                left = n % (2 * units)

                @pl.when(left >= units)
                def _(units=units, left=left):
                    step(n - left, units)

                units //= 2

        sweep(score_step)
        for h in heads:
            rows = pl.ds(h * ROWS, ROWS)
            mx[rows, :] = jnp.broadcast_to(jnp.max(mx[rows, :], axis=1, keepdims=True), (ROWS, 128))

        def value_step(j, units):
            v = jnp.concatenate([vbuf[pl.ds(place(j + i), CHUNK), :] for i in range(units)], axis=0)
            probs = []
            for h in heads:
                rows = pl.ds(h * ROWS, ROWS)
                best = mx[rows, :]
                parts = []
                for g in range(units * CHUNK // 128):
                    p = jnp.exp2(ss[j + g // 2, rows, (g % 2) * 128 : (g % 2 + 1) * 128] - best)
                    parts.append(p.astype(bf16))
                probs.append(jnp.concatenate(parts, axis=1))
                if len(probs) * ROWS == SUB2:
                    acc[pl.ds((h + 1) * ROWS - SUB2, SUB2), :] += lax.dot_general(
                        jnp.concatenate(probs, axis=0), v, (((1,), (0,)), ((), ())), preferred_element_type=f32
                    )
                    probs = []

        sweep(value_step)
        best, sums = jnp.zeros((ROWS, ROWS), f32), jnp.ones((ROWS, ROWS), f32)
        for h in heads:
            rows = pl.ds(h * ROWS, ROWS)
            total = acc[rows, HD:]
            total = jnp.where(total > 0.0, total, 1.0)
            inverse = pl.reciprocal(total, approx=True)
            inverse = inverse * (2.0 - total * inverse)
            o_ref[h // HEADS * 2 + pair, pl.ds((h % HEADS) * ROWS, ROWS), :] = (acc[rows, :HD] * inverse).astype(bf16)
            best = jnp.where(lane == h, mx[rows, :], best)
            sums = jnp.where(lane == h, total, sums)
        stat = (best + jnp.log2(sums)).T
        for i in range(4):
            part = stat[i * HEADS : (i + 1) * HEADS]
            top = part.astype(bf16)
            rest = part - top.astype(f32)
            mid = rest.astype(bf16)
            low = (rest - mid.astype(f32)).astype(bf16)
            o_ref[i * 2 + pair, pl.ds(PIECE, STAT), :] = jnp.concatenate(
                [top.astype(f32), mid.astype(f32), low.astype(f32), jnp.zeros((HEADS, ROWS), f32)], axis=0
            ).astype(bf16)
        return unused

    lax.fori_loop(0, PAIRS, pair_step, 0)


def attend(info, queries, held, got, meta):
    return pl.pallas_call(
        attend_kernel,
        out_shape=jax.ShapeDtypeStruct((GROUP, PIECE + STAT, HD), bf16),
        in_specs=[HBM] + [VMEM] * 6 + [HBM],
        out_specs=VMEM,
        scratch_shapes=[
            pltpu.SMEM((INFO,), i32),
            pltpu.VMEM((META, 128), f32),
            pltpu.SemaphoreType.DMA((2,)),
            pltpu.VMEM((KEYS, HD), bf16),
            pltpu.VMEM((KEYS, 2 * HD), bf16),
            pltpu.VMEM((PAIRS, PROWS, HD), bf16),
            pltpu.VMEM((STEPS, PROWS, CHUNK), f32),
            pltpu.VMEM((PROWS, 128), f32),
            pltpu.VMEM((PROWS, 2 * HD), f32),
        ],
        compiler_params=pltpu.CompilerParams(vmem_limit_bytes=48 * 1024 * 1024),
        cost_estimate=pl.CostEstimate(flops=4 * 8000000 * HD, bytes_accessed=4000000, transcendentals=8000000),
        name="attend",
    )(info, *queries, held, got, meta)


def combine_kernel(r_ref, out_ref):
    parts = []
    for i in range(GROUP):
        stat = r_ref[i, pl.ds(PIECE, STAT), :].astype(f32)
        parts.append(stat[0:4] + stat[4:8] + stat[8:12])
    best = functools.reduce(jnp.maximum, parts)
    weights = [jnp.exp2(part - best) for part in parts]
    total = functools.reduce(jnp.add, weights)
    inverse = 1.0 / total
    table = jnp.concatenate([w * inverse for w in weights] + [jnp.zeros((ROWS - GROUP * HEADS, ROWS), f32)], axis=0).T
    for h in range(HEADS):
        out = jnp.zeros((ROWS, HD), f32)
        for i in range(GROUP):
            at = i * HEADS + h
            out = out + table[:, at : at + 1] * r_ref[i, pl.ds(h * ROWS, ROWS), :].astype(f32)
        out_ref[:, h * HD : (h + 1) * HD] = out.astype(bf16)


def body(queries, new_keys, new_values, cache_keys, cache_values, q_request, block_request):
    across = lax.ppermute(queries, "z0", [(0, 1), (1, 0)])
    slots = pl.pallas_call(
        slots_kernel,
        out_shape=jax.ShapeDtypeStruct((SRC, SLOT, HD), bf16),
        in_specs=[VMEM] * 4,
        out_specs=VMEM,
        cost_estimate=pl.CostEstimate(flops=1000000, bytes_accessed=4000000, transcendentals=0),
        name="slots",
    )(new_keys, new_values, cache_keys, cache_values)
    pair = jnp.concatenate([queries, across], axis=0)
    held = lax.all_to_all(slots, ("y", "zh", "z0"), 0, 0)
    shared = [pair] + [lax.ppermute(pair, ("xh", "xl"), [(i, i ^ d) for i in range(4)]) for d in range(1, 4)]
    meta, info = pl.pallas_call(
        prep_kernel,
        out_shape=(jax.ShapeDtypeStruct((META, 128), f32), jax.ShapeDtypeStruct((INFO,), i32)),
        in_specs=[SMEM, VMEM],
        out_specs=(VMEM, SMEM),
        cost_estimate=pl.CostEstimate(flops=30000000000, bytes_accessed=800000, transcendentals=0),
        compiler_params=pltpu.CompilerParams(vmem_limit_bytes=8 * 1024 * 1024),
        name="prep",
    )(block_request, q_request.reshape(ROWS, ROWS))
    held, meta, info, *shared = lax.optimization_barrier((held, meta, info, *shared))
    got = lax.ppermute(held, "core", [(0, 1), (1, 0)])
    partial = attend(info, shared, held, got, meta)
    parts = lax.all_to_all(partial, ("z0", "xl", "xh"), 0, 0)
    return pl.pallas_call(
        combine_kernel,
        out_shape=jax.ShapeDtypeStruct((ROWS, HEADS * HD), bf16),
        in_specs=[VMEM],
        out_specs=VMEM,
        compiler_params=pltpu.CompilerParams(vmem_limit_bytes=16 * 1024 * 1024),
        name="combine",
    )(parts)


def solution(mesh):
    fine = Mesh(mesh.devices.reshape(2, 8, 4, 2, 2, 2), ("xh", "y", "zh", "z0", "xl", "core"))
    ctx, head = ("xh", "y", "zh", "z0"), ("xl", "core")
    return jax.shard_map(
        body,
        mesh=fine,
        in_specs=(P(ctx, head), P(ctx, None), P(ctx, None), P(ctx, None), P(ctx, None), P(), P()),
        out_specs=P(ctx, head),
        check_vma=False,
    )
```

```python
import functools
import math

import jax
import jax.numpy as jnp
from jax import lax
from jax.experimental import pallas as pl
from jax.experimental.pallas import tpu as pltpu
from jax.sharding import Mesh, PartitionSpec as P

HD = 128
BLK = 16
ROWS = 128
HEADS = 4
SRC = 64
NEWK = 32
OLDK = 16
PER = OLDK // BLK
SLOT = NEWK + OLDK
GROUP = 8
TBS = 4
PAIRS = TBS // 2
SUB1, SUB2 = 256, 256
UNITS = 4
CHUNK = 256
NEW0 = SRC * OLDK + CHUNK
KEYS = NEW0 + SRC * NEWK + CHUNK
STEPS = (SRC * OLDK + SRC * NEWK) // CHUNK
LOW = -1.0e30
SCALE2 = math.log2(math.e) / math.sqrt(HD)
PIECE = HEADS * ROWS
PROWS = 4 * PIECE
STAT = 16
LO0, HI0, CODE0 = 0, TBS * ROWS, 2 * TBS * ROWS
META = CODE0 + (KEYS // 128 + 7) // 8 * 8
BLOCKS = SRC * PER
TB0, INFO = BLOCKS, BLOCKS + 4 * PAIRS

f32, bf16, i32 = jnp.float32, jnp.bfloat16, jnp.int32
VMEM = pl.BlockSpec(memory_space=pltpu.VMEM)
SMEM = pl.BlockSpec(memory_space=pltpu.SMEM)
HBM = pl.BlockSpec(memory_space=pltpu.HBM)


def pick(index, values):
    out = values[-1]
    for at in range(len(values) - 2, -1, -1):
        out = jnp.where(index == at, values[at], out)
    return out


def slots_kernel(new_keys, new_values, cache_keys, cache_values, slots):
    xl, core = lax.axis_index("xl"), lax.axis_index("core")

    def write(new, old):
        for z0 in range(2):
            part = xl * 2 + z0
            fresh = new[pl.ds(pl.multiple_of(part * NEWK, NEWK), NEWK), :]
            cached = old[pl.ds(pl.multiple_of(part * OLDK, OLDK), OLDK), :]
            for i in range(z0, SRC, 2):
                slots[i, :NEWK, :] = fresh
                slots[i, NEWK:, :] = cached

    @pl.when(core == 0)
    def _():
        write(new_keys, cache_keys)

    @pl.when(core == 1)
    def _():
        write(new_values, cache_values)


def prep_kernel(blocks, requests, meta, info):
    xh, y, zh, z0, xl = (lax.axis_index(a) for a in ("xh", "y", "zh", "z0", "xl"))
    part = xl * 2 + z0
    req = requests[...]
    starts = [jnp.int32(0)] + [
        jnp.sum(jnp.where(req < r, 1.0, 0.0).astype(f32)).astype(i32) for r in (1, 2, 3)
    ]

    def count(i, carry):
        r = blocks[(xh * SRC + i // PER) * 4 + part * PER + i % PER]
        return tuple(c + jnp.where(r == k, 1, 0) for k, c in enumerate(carry))

    zero = jnp.int32(0)
    n = lax.fori_loop(0, BLOCKS, count, (zero,) * 4)
    offs = [zero, n[0], n[0] + n[1], n[0] + n[1] + n[2], jnp.int32(BLOCKS)]

    def place(i, carry):
        r = blocks[(xh * SRC + i // PER) * 4 + part * PER + i % PER]
        info[i] = pick(r, carry)
        return tuple(c + jnp.where(r == k, 1, 0) for k, c in enumerate(carry))

    lax.fori_loop(0, BLOCKS, place, tuple(offs[:4]))

    lane = lax.broadcasted_iota(i32, (1, ROWS), 1)
    for pair in range(PAIRS):
        firsts, lasts = [], []
        for e in range(2):
            tb, own = pair * 2 + e, pair * SRC + y * 8 + zh * 2 + e
            row = requests[pl.ds(own, 1), :]
            rowf = row.astype(f32)
            firsts.append(jnp.min(rowf).astype(i32))
            lasts.append(jnp.max(rowf).astype(i32))
            lo = 2 * pick(row, starts)
            hi = 2 * (own * ROWS + lane) + 1
            meta[pl.ds(LO0 + tb * ROWS, ROWS), :] = jnp.broadcast_to(lo.astype(f32), (ROWS, ROWS)).T
            meta[pl.ds(HI0 + tb * ROWS, ROWS), :] = jnp.broadcast_to(hi.astype(f32), (ROWS, ROWS)).T
        first, last = firsts[0], lasts[1]
        clo = pick(first, offs[:4]) * BLK
        chi = pick(last, offs[1:]) * BLK
        cs = (clo >> 7) << 7
        info[TB0 + pair * 4 + 0] = cs
        info[TB0 + pair * 4 + 1] = jnp.where(chi > clo, (chi - cs + CHUNK - 1) // CHUNK, 0)
        base = xh * SRC
        a = jnp.maximum(pick(first, starts) >> 7, base)
        b = jnp.minimum(own, base + SRC - 1)
        ns = (((a - base) * NEWK) >> 7) << 7
        end = (b - base + 1) * NEWK
        info[TB0 + pair * 4 + 2] = NEW0 + ns
        info[TB0 + pair * 4 + 3] = jnp.where(a <= b, (end - ns + CHUNK - 1) // CHUNK, 0)

    shape = (META - CODE0, 128)
    key = lax.broadcasted_iota(i32, shape, 0) * 128 + lax.broadcasted_iota(i32, shape, 1)
    block = key >> 4
    cached = jnp.where(
        block >= offs[3],
        starts[3],
        jnp.where(block >= offs[2], starts[2], jnp.where(block >= offs[1], starts[1], 0)),
    )
    u = key - NEW0
    fresh = ROWS * (xh * SRC + (u >> 5)) + NEWK * part + (u & (NEWK - 1))
    code = jnp.where(key < SRC * OLDK, 2 * cached, -1)
    code = jnp.where((u >= 0) & (u < SRC * NEWK), 2 * fresh + 1, code)
    meta[pl.ds(CODE0, META - CODE0), :] = code.astype(f32)


def attend_kernel(info_in, *refs):
    q_refs, refs = refs[:4], refs[4:]
    own_ref, got_ref, meta_in, o_ref, info, meta, sem, kbuf, vbuf, qs, ss, mx, acc = refs
    copy_info = pltpu.make_async_copy(info_in, info, sem.at[0])
    copy_meta = pltpu.make_async_copy(meta_in, meta, sem.at[1])
    copy_info.start()
    copy_meta.start()
    for at in (SRC * OLDK, KEYS - CHUNK):
        kbuf[pl.ds(at, CHUNK), :] = jnp.zeros((CHUNK, HD), bf16)
        vbuf[pl.ds(at, CHUNK), :HD] = jnp.zeros((CHUNK, HD), bf16)
    vbuf[:, HD:] = jnp.ones((KEYS, HD), bf16)
    xh, z0, xl, core = (lax.axis_index(a) for a in ("xh", "z0", "xl", "core"))
    for d in range(4):
        for e in range(2):
            for h in range(HEADS):
                at = pl.multiple_of(((z0 ^ e) * 2 + (xl ^ (d & 1))) * PIECE + h * ROWS, ROWS)
                qs[xh ^ (d >> 1), pl.ds(at, ROWS), :] = q_refs[d][pl.ds(e * ROWS, ROWS), h * HD : (h + 1) * HD]

    copy_info.wait()

    def fill(buf, ref):
        buf[pl.ds(NEW0, SRC * NEWK), :HD] = ref[:, :NEWK, :].reshape(SRC * NEWK, HD)
        for i in range(BLOCKS):
            to = pl.multiple_of(info[i] * BLK, BLK)
            buf[pl.ds(to, BLK), :HD] = ref[i // PER, pl.ds(NEWK + (i % PER) * BLK, BLK), :]

    @pl.when(core == 0)
    def _():
        fill(kbuf, own_ref)
        fill(vbuf, got_ref)

    @pl.when(core == 1)
    def _():
        fill(kbuf, got_ref)
        fill(vbuf, own_ref)

    lane = lax.broadcasted_iota(i32, (ROWS, ROWS), 1)
    heads = range(4 * HEADS)
    copy_meta.wait()

    def pair_step(pair, unused):
        cs, nc, ns, nn = (info[TB0 + pair * 4 + i] for i in range(4))

        @pl.when(nc + nn == 0)
        def _():
            mx[...] = jnp.full(mx.shape, LOW, f32)
            acc[...] = jnp.zeros(acc.shape, f32)


        def place(j):
            return pl.multiple_of(jnp.where(j < nc, cs + j * CHUNK, ns + (j - nc) * CHUNK), 128)

        def score_step(j, units):
            keys, bias = [], ([], [])
            for i in range(units):
                at = place(j + i)
                keys.append(kbuf[pl.ds(at, CHUNK), :])
                for g in range(CHUNK // 128):
                    code = meta[pl.ds(CODE0 + (at >> 7) + g, 1), :]
                    for e in range(2):
                        line = (pair * 2 + e) * ROWS
                        lo = meta[pl.ds(pl.multiple_of(LO0 + line, ROWS), ROWS), :]
                        hi = meta[pl.ds(pl.multiple_of(HI0 + line, ROWS), ROWS), :]
                        bias[e].append(jnp.where((code >= lo) & (code <= hi), 0.0, LOW))
            keys = jnp.concatenate(keys, axis=0)
            for h in heads:
                low = h * ROWS % SUB1
                if low == 0:
                    s = lax.dot_general(
                        qs[pair, pl.ds(h * ROWS, SUB1), :], keys, (((1,), (1,)), ((), ())), preferred_element_type=f32
                    )
                rows = pl.ds(h * ROWS, ROWS)
                best = jnp.where(j == 0, LOW, mx[rows, :])
                for g in range(units * CHUNK // 128):
                    part = s[low : low + ROWS, g * 128 : (g + 1) * 128] * SCALE2 + bias[h // 8][g]
                    ss[j + g // 2, rows, (g % 2) * 128 : (g % 2 + 1) * 128] = part
                    best = jnp.maximum(best, part)
                mx[rows, :] = best

        def sweep(step):
            n = nc + nn

            def most(i, unused):
                step(i * UNITS, UNITS)
                return unused

            lax.fori_loop(0, n // UNITS, most, 0)
            units = UNITS // 2
            while units:
                left = n % (2 * units)

                @pl.when(left >= units)
                def _(units=units, left=left):
                    step(n - left, units)

                units //= 2

        sweep(score_step)
        for h in heads:
            rows = pl.ds(h * ROWS, ROWS)
            mx[rows, :] = jnp.broadcast_to(jnp.max(mx[rows, :], axis=1, keepdims=True), (ROWS, 128))

        def value_step(j, units):
            v = jnp.concatenate([vbuf[pl.ds(place(j + i), CHUNK), :] for i in range(units)], axis=0)
            probs = []
            for h in heads:
                rows = pl.ds(h * ROWS, ROWS)
                best = mx[rows, :]
                parts = []
                for g in range(units * CHUNK // 128):
                    p = jnp.exp2(ss[j + g // 2, rows, (g % 2) * 128 : (g % 2 + 1) * 128] - best)
                    parts.append(p.astype(bf16))
                probs.append(jnp.concatenate(parts, axis=1))
                if len(probs) * ROWS == SUB2:
                    some = pl.ds((h + 1) * ROWS - SUB2, SUB2)
                    acc[some, :] = jnp.where(j == 0, 0.0, acc[some, :]) + lax.dot_general(
                        jnp.concatenate(probs, axis=0), v, (((1,), (0,)), ((), ())), preferred_element_type=f32
                    )
                    probs = []

        sweep(value_step)
        best, sums = jnp.zeros((ROWS, ROWS), f32), jnp.ones((ROWS, ROWS), f32)
        for h in heads:
            rows = pl.ds(h * ROWS, ROWS)
            total = acc[rows, HD:]
            total = jnp.where(total > 0.0, total, 1.0)
            inverse = pl.reciprocal(total, approx=True)
            inverse = inverse * (2.0 - total * inverse)
            o_ref[h // HEADS * 2 + pair, pl.ds((h % HEADS) * ROWS, ROWS), :] = (acc[rows, :HD] * inverse).astype(bf16)
            best = jnp.where(lane == h, mx[rows, :], best)
            sums = jnp.where(lane == h, total, sums)
        stat = (best + jnp.log2(sums)).T
        for i in range(4):
            part = stat[i * HEADS : (i + 1) * HEADS]
            top = part.astype(bf16)
            rest = part - top.astype(f32)
            mid = rest.astype(bf16)
            low = (rest - mid.astype(f32)).astype(bf16)
            o_ref[i * 2 + pair, pl.ds(PIECE, STAT), :] = jnp.concatenate(
                [top.astype(f32), mid.astype(f32), low.astype(f32), jnp.zeros((HEADS, ROWS), f32)], axis=0
            ).astype(bf16)
        return unused

    lax.fori_loop(0, PAIRS, pair_step, 0)


def attend(info, queries, held, got, meta):
    return pl.pallas_call(
        attend_kernel,
        out_shape=jax.ShapeDtypeStruct((GROUP, PIECE + STAT, HD), bf16),
        in_specs=[HBM] + [VMEM] * 6 + [HBM],
        out_specs=VMEM,
        scratch_shapes=[
            pltpu.SMEM((INFO,), i32),
            pltpu.VMEM((META, 128), f32),
            pltpu.SemaphoreType.DMA((2,)),
            pltpu.VMEM((KEYS, HD), bf16),
            pltpu.VMEM((KEYS, 2 * HD), bf16),
            pltpu.VMEM((PAIRS, PROWS, HD), bf16),
            pltpu.VMEM((STEPS, PROWS, CHUNK), f32),
            pltpu.VMEM((PROWS, 128), f32),
            pltpu.VMEM((PROWS, 2 * HD), f32),
        ],
        compiler_params=pltpu.CompilerParams(vmem_limit_bytes=48 * 1024 * 1024),
        cost_estimate=pl.CostEstimate(flops=4 * 8000000 * HD, bytes_accessed=4000000, transcendentals=8000000),
        name="attend",
    )(info, *queries, held, got, meta)


def combine_kernel(r_ref, out_ref):
    parts = []
    for i in range(GROUP):
        stat = r_ref[i, pl.ds(PIECE, STAT), :].astype(f32)
        parts.append(stat[0:4] + stat[4:8] + stat[8:12])
    best = functools.reduce(jnp.maximum, parts)
    weights = [jnp.exp2(part - best) for part in parts]
    total = functools.reduce(jnp.add, weights)
    inverse = 1.0 / total
    table = jnp.concatenate([w * inverse for w in weights] + [jnp.zeros((ROWS - GROUP * HEADS, ROWS), f32)], axis=0).T
    for h in range(HEADS):
        out = jnp.zeros((ROWS, HD), f32)
        for i in range(GROUP):
            at = i * HEADS + h
            out = out + table[:, at : at + 1] * r_ref[i, pl.ds(h * ROWS, ROWS), :].astype(f32)
        out_ref[:, h * HD : (h + 1) * HD] = out.astype(bf16)


def body(queries, new_keys, new_values, cache_keys, cache_values, q_request, block_request):
    across = lax.ppermute(queries, "z0", [(0, 1), (1, 0)])
    slots = pl.pallas_call(
        slots_kernel,
        out_shape=jax.ShapeDtypeStruct((SRC, SLOT, HD), bf16),
        in_specs=[VMEM] * 4,
        out_specs=VMEM,
        cost_estimate=pl.CostEstimate(flops=1000000, bytes_accessed=4000000, transcendentals=0),
        name="slots",
    )(new_keys, new_values, cache_keys, cache_values)
    pair = jnp.concatenate([queries, across], axis=0)
    held = lax.all_to_all(slots, ("y", "zh", "z0"), 0, 0)
    shared = [pair] + [lax.ppermute(pair, ("xh", "xl"), [(i, i ^ d) for i in range(4)]) for d in range(1, 4)]
    meta, info = pl.pallas_call(
        prep_kernel,
        out_shape=(jax.ShapeDtypeStruct((META, 128), f32), jax.ShapeDtypeStruct((INFO,), i32)),
        in_specs=[SMEM, VMEM],
        out_specs=(VMEM, SMEM),
        cost_estimate=pl.CostEstimate(flops=30000000000, bytes_accessed=800000, transcendentals=0),
        compiler_params=pltpu.CompilerParams(vmem_limit_bytes=8 * 1024 * 1024),
        name="prep",
    )(block_request, q_request.reshape(ROWS, ROWS))
    held, meta, info, *shared = lax.optimization_barrier((held, meta, info, *shared))
    got = lax.ppermute(held, "core", [(0, 1), (1, 0)])
    partial = attend(info, shared, held, got, meta)
    parts = lax.all_to_all(partial, ("z0", "xl", "xh"), 0, 0)
    return pl.pallas_call(
        combine_kernel,
        out_shape=jax.ShapeDtypeStruct((ROWS, HEADS * HD), bf16),
        in_specs=[VMEM],
        out_specs=VMEM,
        compiler_params=pltpu.CompilerParams(vmem_limit_bytes=16 * 1024 * 1024),
        name="combine",
    )(parts)


def solution(mesh):
    fine = Mesh(mesh.devices.reshape(2, 8, 4, 2, 2, 2), ("xh", "y", "zh", "z0", "xl", "core"))
    ctx, head = ("xh", "y", "zh", "z0"), ("xl", "core")
    return jax.shard_map(
        body,
        mesh=fine,
        in_specs=(P(ctx, head), P(ctx, None), P(ctx, None), P(ctx, None), P(ctx, None), P(), P()),
        out_specs=P(ctx, head),
        check_vma=False,
    )
```
